32 devices in a mesh: groups: 1, expert: 32 (over z, y, x, core), dp: 1.
Axes of the slice: x: 2, y: 2, z: 4, core: 2. Of those that a mesh axis runs over, the one named last changes fastest.
Arguments:
- grad_out: bfloat16 [4096, 1024], P(('groups', 'expert', 'dp')), may hold values from -6 to 6
- gates: float32 [4096, 8], P(('groups', 'expert', 'dp')), may hold values from 0.05 to 1
- expert_ids: int32 [4096, 8], P(('groups', 'expert', 'dp')), may hold values from 0 to 31, as said below
- pre_acts: bfloat16 [4096, 8, 768], P(('groups', 'expert', 'dp')), may hold values from -8 to 8
- w2: bfloat16 [32, 384, 1024], P('expert', None, 'dp'), may hold values from -0.1875 to 0.1875
Outputs:
- pre_grad: bfloat16 [4096, 8, 768], P(('groups', 'expert', 'dp'))
- w2_grad: bfloat16 [32, 384, 1024], P('expert', 'groups', 'dp')
The draws below stay inside these ranges and needn't reach their ends.
Inputs may be any that keep to these rules, and one draw needn't show every extreme that they name: `expert_ids`: each token names 8 different experts. There is a hot list of 2 experts, the same for all devices of a part, that the 128 tokens of every device name exactly 64 times each; every other expert is named at most 31 times by one device's tokens, and in every draw one of them is named exactly 31 times by every device's tokens.
All inputs are finite; a program needn't handle non-finite values.
Results may differ from the reference program's by a relative error of at most 0.0057.
Values may be sent and summed in bfloat16 or wider, within the bound.
No kernel may reach another device: no remote copies, remote signals or barrier semaphores. Data moves between devices by JAX's collectives and lax.ppermute only.
A program may use at most 128 MiB of HBM per device.

```python
import math
import jax
import jax.numpy as jnp
from jax import lax

DW = 1024
HW = 384
TOPK = 8
HOT = 2
TOK_DEV = 128
EXPERTS = 32
CAP = 64
COLD_CAP = 31
TOKENS = 4096
N_EXPERT = 32
N_DP = 1


def draw_expert_ids(key, part):
    key = jax.random.fold_in(key, 11)
    device_count = TOKENS // TOK_DEV
    rows_device = TOK_DEV * TOPK
    cold_count = EXPERTS - HOT
    order = jax.random.permutation(jax.random.fold_in(key, 1), EXPERTS).astype(jnp.int32)
    hot_list = order[:HOT]
    cold_list = order[HOT:]
    rest_rows = rows_device - HOT * CAP - COLD_CAP
    spare = jnp.repeat(jnp.arange(1, cold_count, dtype=jnp.int32), COLD_CAP)
    hot_part = jnp.repeat(hot_list, CAP)

    def one_device(device_key):
        first_key, second_key, third_key = jax.random.split(device_key, 3)
        chosen = jax.random.permutation(first_key, spare)[:rest_rows]
        tickets = jnp.sort(jnp.concatenate([jnp.zeros((COLD_CAP,), jnp.int32), chosen]))
        listing = jnp.concatenate([hot_part, cold_list[tickets]])
        table = listing.reshape(TOPK, TOK_DEV).T
        table = table[jax.random.permutation(second_key, TOK_DEV)]
        offset = jax.random.randint(third_key, (TOK_DEV, 1), 0, TOPK).astype(jnp.int32)
        columns = (jnp.arange(TOPK, dtype=jnp.int32)[None, :] + offset) % TOPK
        return jnp.take_along_axis(table, columns, 1)
    device_keys = jax.random.split(jax.random.fold_in(key, 2), device_count)
    return jax.vmap(one_device)(device_keys).reshape(TOKENS, TOPK).astype(jnp.int32)


def steps_of(own_key, dims, shards, least, high):
    def one(dim, parts):
        draws = jax.random.uniform(jax.random.fold_in(jax.random.fold_in(own_key, 6), dim), (parts,), jnp.float32, least / len(shards), high / len(shards))
        return jnp.repeat(jnp.exp(draws), dims[dim] // parts).reshape((-1,) + (1,) * (len(dims) - dim - 1))

    level = one(*shards[0])
    for cut in shards[1:]:
        level = level * one(*cut)
    return level


def bell_draw(own_key, shape, width, limit, shards=(), kind=jnp.bfloat16):
    entries = jax.random.normal(own_key, shape, jnp.float32) * width
    if len(shards) > 0:
        entries = steps_of(own_key, shape, shards, -0.22, 0.18) * entries
    return jnp.clip(entries, min=-limit, max=limit).astype(kind)


def setup_inputs(seed: int = 0, part: int = 0) -> dict:
    seeds = jax.random.split(jax.random.key(seed), 6)
    part_splits = jax.random.split(jax.random.fold_in(seeds[5], part), 6)
    grad_out = bell_draw(part_splits[0], (TOKENS, DW), 1.0, 6.0, ((0, 32),))
    gates = jnp.clip(jnp.exp(math.log(1.0) - 2.9957323 * jax.random.uniform(part_splits[1], (TOKENS, TOPK), jnp.float32) ** steps_of(part_splits[1], (TOKENS, TOPK), ((0, 32),), -0.2, 0.2)), 0.05, 1.0)
    expert_ids = draw_expert_ids(jax.random.fold_in(jax.random.fold_in(seeds[5], part), 71), part)
    pre_acts = bell_draw(part_splits[3], (TOKENS, TOPK, 2 * HW), 1.5, 8.0, ((0, 32),))
    w2 = bell_draw(seeds[4], (EXPERTS, HW, DW), DW ** -0.5, 0.1875, ((0, 32),))
    return dict(grad_out=grad_out, gates=gates, expert_ids=expert_ids, pre_acts=pre_acts, w2=w2)


def silu_parts(gate_pre):
    sigma = jax.nn.sigmoid(gate_pre)
    return gate_pre * sigma, sigma * (1.0 + gate_pre * (1.0 - sigma))


def reference(grad_out, gates, expert_ids, pre_acts, w2):
    row_count = TOKENS * TOPK
    grad_rows = (gates[:, :, None] * grad_out[:, None, :].astype(jnp.float32)).astype(jnp.bfloat16).reshape(row_count, DW)
    flat_pre = pre_acts.reshape(row_count, 2 * HW)
    gate_pre = flat_pre[:, :HW].astype(jnp.float32)
    up_pre = flat_pre[:, HW:].astype(jnp.float32)
    activation, slopes = silu_parts(gate_pre)
    hidden = (activation * up_pre).astype(jnp.bfloat16)
    flat_ids = expert_ids.reshape(row_count).astype(jnp.int32)
    sort_order = jnp.argsort(flat_ids, stable=True).astype(jnp.int32)
    sorted_ids = flat_ids[sort_order]
    expert_range = jnp.arange(EXPERTS, dtype=jnp.int32)
    starts = jnp.searchsorted(sorted_ids, expert_range).astype(jnp.int32)
    finish = jnp.searchsorted(sorted_ids, expert_range, side="right").astype(jnp.int32)
    block_rows = N_EXPERT * N_DP * CAP
    sorted_grad = jnp.concatenate([grad_rows[sort_order], jnp.zeros((block_rows, DW), jnp.bfloat16)], 0)
    sorted_hidden = jnp.concatenate([hidden[sort_order], jnp.zeros((block_rows, HW), jnp.bfloat16)], 0)

    def per_expert(expert):
        start = starts[expert]
        grad_block = lax.dynamic_slice_in_dim(sorted_grad, start, block_rows, 0)
        hidden_block = lax.dynamic_slice_in_dim(sorted_hidden, start, block_rows, 0)
        live = jnp.arange(block_rows, dtype=jnp.int32) < (finish[expert] - start)
        hidden_block = jnp.where(live[:, None], hidden_block, jnp.zeros_like(hidden_block))
        weight = w2[expert]
        slope_block = lax.dot_general(grad_block, weight, (((1,), (1,)), ((), ())), preferred_element_type=jnp.float32)
        weight_grad = lax.dot_general(hidden_block, grad_block, (((0,), (0,)), ((), ())), preferred_element_type=jnp.float32)
        return slope_block, weight_grad

    slope_blocks, weight_grads = lax.map(per_expert, expert_range)
    offsets = jnp.arange(row_count, dtype=jnp.int32) - starts[sorted_ids]
    sorted_slope = slope_blocks[sorted_ids, offsets]
    hidden_grad = jnp.zeros((row_count, HW), jnp.float32).at[sort_order].set(sorted_slope)
    pre_grad = jnp.concatenate([hidden_grad * up_pre * slopes, hidden_grad * activation], 1)
    pre_grad = pre_grad.astype(jnp.bfloat16).reshape(TOKENS, TOPK, 2 * HW)
    return pre_grad, weight_grads.astype(jnp.bfloat16)
```

```python
import jax
import jax.numpy as jnp
from jax import lax
from jax.experimental import pallas as pl
from jax.experimental.pallas import tpu as pltpu
from jax.sharding import PartitionSpec as P

X_BIT, Y_BIT, CORE_BIT = 2, 4, 1
PLANE = (0, X_BIT, Y_BIT, X_BIT | Y_BIT)
ID_ROWS = 16
VMEM_BYTES = 56 * 1024 * 1024
F32, BF16 = jnp.float32, jnp.bfloat16


def params(steps=1):
    return pltpu.CompilerParams(
        dimension_semantics=("arbitrary",) * steps, vmem_limit_bytes=VMEM_BYTES
    )


def cost(flops, moved):
    return pl.CostEstimate(flops=flops, bytes_accessed=moved, transcendentals=0)


def swap(value, bit):
    count = lax.axis_size("expert")
    return lax.ppermute(value, "expert", [(j, j ^ bit) for j in range(count)])


def iota_f32(shape, dim):
    return lax.broadcasted_iota(jnp.int32, shape, dim).astype(F32)


def pack_kernel(cap, ids_ref, gates_ref, pre_ref, out_ref, place_ref, hidden, place):
    step = pl.program_id(0)
    members = pl.num_programs(0)
    rows = ids_ref.shape[1]
    width = hidden.shape[1]

    @pl.when(step == 0)
    def _():
        gate_pre = pre_ref[:, :width].astype(F32)
        up_pre = pre_ref[:, width:].astype(F32)
        value = gate_pre * jax.nn.sigmoid(gate_pre) * up_pre
        hidden[...] = (value * gates_ref[...]).astype(BF16)
        ids = ids_ref[...]
        member = (ids >> 3) * 2 + (ids & 1)
        own = lax.broadcasted_iota(jnp.int32, (members, rows), 0) == member
        before = lax.broadcasted_iota(jnp.int32, (rows, rows), 0) < lax.broadcasted_iota(
            jnp.int32, (rows, rows), 1
        )
        rank = jnp.dot(
            own.astype(F32).astype(BF16),
            before.astype(F32).astype(BF16),
            preferred_element_type=F32,
        )
        slot = jnp.sum(jnp.where(own, rank, 0.0), 0, keepdims=True)
        where = member * cap + slot.astype(jnp.int32)
        place[...] = where
        place_ref[...] = where

    wanted = lax.broadcasted_iota(jnp.int32, (cap, rows), 0) + step * cap
    pick = (wanted == place[...]).astype(F32).astype(BF16)
    out_ref[0] = jnp.dot(pick, hidden[...], preferred_element_type=F32).astype(BF16)


def pack_hidden(ids, gate_column, flat_pre, members, cap):
    rows, both = flat_pre.shape
    width = both // 2
    return pl.pallas_call(
        lambda *refs: pack_kernel(cap, *refs),
        grid=(members,),
        in_specs=[
            pl.BlockSpec((1, rows), lambda q: (0, 0)),
            pl.BlockSpec((rows, 1), lambda q: (0, 0)),
            pl.BlockSpec((rows, both), lambda q: (0, 0)),
        ],
        out_specs=[
            pl.BlockSpec((1, cap, width), lambda q: (q, 0, 0)),
            pl.BlockSpec((1, rows), lambda q: (0, 0)),
        ],
        out_shape=[
            jax.ShapeDtypeStruct((members, cap, width), BF16),
            jax.ShapeDtypeStruct((1, rows), jnp.int32),
        ],
        scratch_shapes=[pltpu.VMEM((rows, width), BF16), pltpu.VMEM((1, rows), jnp.int32)],
        compiler_params=params(),
        cost_estimate=cost(2 * members * cap * rows * width, 2 * rows * both),
    )(ids, gate_column, flat_pre)


def picks(ids, me, cap):
    top, tokens = ids.shape
    experts = [(me ^ mask).astype(F32) for mask in PLANE]
    hits = [(ids == expert).astype(F32) for expert in experts]
    any_hit = hits[0] + hits[1] + hits[2] + hits[3]
    earlier = []
    total = jnp.zeros((1, tokens), F32)
    for k in range(top):
        earlier.append(total)
        total = total + any_hit[k : k + 1]
    before = iota_f32((tokens, tokens), 0) < iota_f32((tokens, tokens), 1)
    base = jnp.dot(
        jnp.broadcast_to(total, (8, tokens)).astype(BF16),
        before.astype(F32).astype(BF16),
        preferred_element_type=F32,
    )[:1]
    rank = base + jnp.concatenate(earlier, 0) + 1.0
    row = iota_f32((cap, tokens), 0) + 1.0
    parts = []
    for hit in hits:
        slot = jnp.sum(hit * rank, 0, keepdims=True)
        parts.append((row == slot).astype(F32).astype(BF16))
    return jnp.concatenate(parts, 1)


def source_ids(block, tokens, top):
    return block[tokens : tokens + ID_ROWS, :tokens].astype(F32)[:top]


def slope_kernel(cap, tokens, top, info, near_ref, far_ref, w0, w1, w2, w3a, w3b, out_ref):
    me = info[0]
    core = me & 1
    near, far = near_ref[...], far_ref[...]
    grads = jnp.concatenate([near[:tokens], far[:tokens]], 0)
    weights = (w0[...], w1[...], w2[...], jnp.concatenate([w3a[...], w3b[...]], 0))
    slopes = [
        lax.dot_general(
            grads, weight, (((1,), (1,)), ((), ())), preferred_element_type=F32
        ).astype(BF16)
        for weight in weights
    ]
    for side, block in enumerate((near, far)):
        pick = picks(source_ids(block, tokens, top), me, cap)
        stacked = jnp.concatenate(
            [slope[side * tokens : (side + 1) * tokens] for slope in slopes], 0
        )
        packed = jnp.dot(pick, stacked, preferred_element_type=F32).astype(BF16)
        out_ref[core if side == 0 else 1 - core] = packed


def packed_slopes(info, near, far, weights, cap, tokens, top):
    block_rows = tokens + ID_ROWS
    blocks = near.shape[0] // block_rows
    model = near.shape[1]
    width = weights[0].shape[0]
    whole = lambda w: pl.BlockSpec(w.shape, lambda j, s: (0, 0))
    return pl.pallas_call(
        lambda *refs: slope_kernel(cap, tokens, top, *refs),
        grid_spec=pltpu.PrefetchScalarGridSpec(
            num_scalar_prefetch=1,
            grid=(blocks,),
            in_specs=[
                pl.BlockSpec((block_rows, model), lambda j, s: (j, 0)),
                pl.BlockSpec((block_rows, model), lambda j, s: (j, 0)),
            ]
            + [whole(w) for w in weights],
            out_specs=pl.BlockSpec((2, cap, width), lambda j, s: (s[1 + j], 0, 0)),
        ),
        out_shape=jax.ShapeDtypeStruct((2 * blocks, cap, width), BF16),
        compiler_params=params(),
        cost_estimate=cost(2 * 2 * blocks * tokens * model * 4 * width, 4 * near.size),
    )(info, near, far, *weights)


def weight_kernel(
    cap, tokens, top, info, near_ref, far_ref, hidden_ref, own_ref, x_ref, y_ref, xk_ref, yk_ref, spread, grads
):
    me = info[0]
    core = me & 1
    block_rows = tokens + ID_ROWS
    blocks = near_ref.shape[0] // block_rows
    width = hidden_ref.shape[2]
    half = width // 2

    def fill(j, carry):
        for side, ref in enumerate((near_ref, far_ref)):
            start = pl.multiple_of(j * block_rows, ID_ROWS)
            block = ref[pl.ds(start, block_rows), :]
            pick = picks(source_ids(block, tokens, top), me, cap)
            member = info[1 + j] * 2 + (core if side == 0 else 1 - core)
            arrived = hidden_ref[member].astype(F32).T.astype(BF16)
            wide = jnp.dot(arrived, pick, preferred_element_type=F32).astype(BF16)
            at = pl.multiple_of((side * blocks + j) * tokens, tokens)
            for e in range(4):
                spread[pl.ds(e * width, width), pl.ds(at, tokens)] = wide[
                    :, e * tokens : (e + 1) * tokens
                ]
            grads[pl.ds(at, tokens), :] = block[:tokens]
        return carry

    lax.fori_loop(0, blocks, fill, 0)

    def product(expert, first, count):
        at = expert * width + first
        return jnp.dot(
            spread[at : at + count, :], grads[...], preferred_element_type=F32
        )

    x_ref[:half] = product(1, 0, half).astype(BF16)
    x_ref[half:] = product(3, 0, half).astype(BF16)
    y_ref[:half] = product(2, half, half).astype(BF16)
    y_ref[half:] = product(3, half, half).astype(BF16)
    own_ref[...] = product(0, 0, width)
    xk_ref[...] = product(1, half, half).astype(BF16)
    yk_ref[...] = product(2, 0, half).astype(BF16)


def weight_partials(info, near, far, hidden, cap, tokens, top):
    blocks = near.shape[0] // (tokens + ID_ROWS)
    model = near.shape[1]
    width = hidden.shape[2]
    half = width // 2
    every = 2 * blocks * tokens
    vmem = pl.BlockSpec(memory_space=pltpu.VMEM)
    return pl.pallas_call(
        lambda *refs: weight_kernel(cap, tokens, top, *refs),
        in_specs=[pl.BlockSpec(memory_space=pltpu.SMEM), vmem, vmem, vmem],
        out_specs=[vmem] * 5,
        out_shape=[
            jax.ShapeDtypeStruct((width, model), F32),
            jax.ShapeDtypeStruct((width, model), BF16),
            jax.ShapeDtypeStruct((width, model), BF16),
            jax.ShapeDtypeStruct((half, model), BF16),
            jax.ShapeDtypeStruct((half, model), BF16),
        ],
        scratch_shapes=[pltpu.VMEM((4 * width, every), BF16), pltpu.VMEM((every, model), BF16)],
        compiler_params=params(0),
        cost_estimate=cost(2 * every * model * 4 * width, 4 * near.size),
    )(info, near, far, hidden)


def finish_kernel(place_ref, gates_ref, pre_ref, back_ref, out_ref):
    rows, both = pre_ref.shape
    width = both // 2
    slots = back_ref.shape[0]
    pick = lax.broadcasted_iota(jnp.int32, (rows, slots), 1) == place_ref[...]
    slope = jnp.dot(
        pick.astype(F32).astype(BF16), back_ref[...], preferred_element_type=F32
    )
    slope = slope * gates_ref[...]
    gate_pre = pre_ref[:, :width].astype(F32)
    up_pre = pre_ref[:, width:].astype(F32)
    sigma = jax.nn.sigmoid(gate_pre)
    out_ref[:, :width] = (
        slope * up_pre * (sigma * (1.0 + gate_pre * (1.0 - sigma)))
    ).astype(BF16)
    out_ref[:, width:] = (slope * (gate_pre * sigma)).astype(BF16)


def finish(place, gate_column, flat_pre, back):
    rows, both = flat_pre.shape
    tile = rows // 4
    return pl.pallas_call(
        finish_kernel,
        grid=(4,),
        in_specs=[
            pl.BlockSpec((tile, 1), lambda i: (i, 0)),
            pl.BlockSpec((tile, 1), lambda i: (i, 0)),
            pl.BlockSpec((tile, both), lambda i: (i, 0)),
            pl.BlockSpec(back.shape, lambda i: (0, 0)),
        ],
        out_specs=pl.BlockSpec((tile, both), lambda i: (i, 0)),
        out_shape=jax.ShapeDtypeStruct((rows, both), BF16),
        compiler_params=params(),
        cost_estimate=cost(2 * rows * both * back.shape[0], 4 * rows * both),
    )(place, gate_column, flat_pre, back)


def per_device(grad_out, gates, expert_ids, pre_acts, w2):
    count = lax.axis_size("expert")
    me = lax.axis_index("expert")
    tokens, top = expert_ids.shape
    model = grad_out.shape[1]
    width = w2.shape[1]
    half = width // 2
    rows = tokens * top
    members = count // 4
    hot = 2 * rows // count
    cold = (rows - 2 * hot) // (count - 2) + 2
    cap = -(-(2 * hot + 2 * cold) // 16) * 16
    groups = [[j for j in range(count) if j & 6 == mask] for mask in PLANE]

    def exchange(chunks):
        return lax.all_to_all(
            chunks, "expert", split_axis=0, concat_axis=0, tiled=True, axis_index_groups=groups
        )

    id_rows = jnp.zeros((ID_ROWS, model), BF16)
    id_rows = lax.dynamic_update_slice(id_rows, expert_ids.T.astype(BF16), (0, 0))
    near = jnp.concatenate([grad_out, id_rows], 0)
    masks = [0]
    bit = count // 2
    while bit >= 8:
        near = jnp.concatenate([near, swap(near, bit)], 0)
        masks = masks + [mask ^ bit for mask in masks]
        bit //= 2
    far = swap(near, CORE_BIT)
    info = jnp.stack([me] + [(me ^ mask) // 8 for mask in masks]).astype(jnp.int32)

    own_w = lax.all_gather(w2, "dp", axis=2, tiled=True)[0]
    x_w, y_w = swap(own_w, X_BIT), swap(own_w, Y_BIT)
    diag_a, diag_b = swap(x_w[:half], Y_BIT), swap(y_w[half:], X_BIT)

    flat_pre = pre_acts.reshape(rows, 2 * width)
    gate_column = gates.reshape(rows, 1)
    packed, place = pack_hidden(expert_ids.reshape(1, rows), gate_column, flat_pre, members, cap)
    arrived = exchange(packed)

    slopes = packed_slopes(info, near, far, (own_w, x_w, y_w, diag_a, diag_b), cap, tokens, top)
    back = exchange(slopes).reshape(members * cap, width)

    own, x_send, y_send, x_keep, y_keep = weight_partials(
        info, near, far, arrived, cap, tokens, top
    )
    from_x, from_y = swap(x_send, X_BIT), swap(y_send, Y_BIT)
    to_y = (y_keep.astype(F32) + from_x[half:].astype(F32)).astype(BF16)
    to_x = (x_keep.astype(F32) + from_y[half:].astype(F32)).astype(BF16)
    last_a, last_b = swap(to_y, Y_BIT), swap(to_x, X_BIT)
    total = own + jnp.concatenate(
        [
            from_x[:half].astype(F32) + last_a.astype(F32),
            from_y[:half].astype(F32) + last_b.astype(F32),
        ],
        0,
    )
    total = lax.psum_scatter(total, "dp", scatter_dimension=1, tiled=True)

    pre_grad = finish(place.reshape(rows, 1), gate_column, flat_pre, back)
    return pre_grad.reshape(tokens, top, 2 * width), total[None].astype(BF16)


def solution(mesh):
    in_specs = (
        P(("groups", "expert", "dp"), None),
        P(("groups", "expert", "dp"), None),
        P(("groups", "expert", "dp"), None),
        P(("groups", "expert", "dp"), None, None),
        P("expert", None, "dp"),
    )
    out_specs = (P(("groups", "expert", "dp"), None, None), P("expert", "groups", "dp"))
    return jax.shard_map(
        per_device, mesh=mesh, in_specs=in_specs, out_specs=out_specs, check_vma=False
    )
```

```python
import jax
import jax.numpy as jnp
from jax import lax
from jax.experimental import pallas as pl
from jax.experimental.pallas import tpu as pltpu
from jax.sharding import PartitionSpec as P

X_BIT, Y_BIT, CORE_BIT = 2, 4, 1
PLANE = (0, X_BIT, Y_BIT, X_BIT | Y_BIT)
ID_ROWS = 16
VMEM_BYTES = 56 * 1024 * 1024
F32, BF16 = jnp.float32, jnp.bfloat16


def params(steps=1):
    return pltpu.CompilerParams(
        dimension_semantics=("arbitrary",) * steps, vmem_limit_bytes=VMEM_BYTES
    )


def cost(flops, moved):
    return pl.CostEstimate(flops=flops, bytes_accessed=moved, transcendentals=0)


def swap(value, bit):
    count = lax.axis_size("expert")
    return lax.ppermute(value, "expert", [(j, j ^ bit) for j in range(count)])


def iota_f32(shape, dim):
    return lax.broadcasted_iota(jnp.int32, shape, dim).astype(F32)


def pack_kernel(cap, ids_ref, gates_ref, pre_ref, out_ref, place_ref, hidden, place):
    step = pl.program_id(0)
    members = pl.num_programs(0)
    rows = ids_ref.shape[1]
    width = hidden.shape[1]

    @pl.when(step == 0)
    def _():
        gate_pre = pre_ref[:, :width].astype(F32)
        up_pre = pre_ref[:, width:].astype(F32)
        value = gate_pre * jax.nn.sigmoid(gate_pre) * up_pre
        hidden[...] = (value * gates_ref[...]).astype(BF16)
        ids = ids_ref[...]
        member = (ids >> 3) * 2 + (ids & 1)
        own = lax.broadcasted_iota(jnp.int32, (members, rows), 0) == member
        before = lax.broadcasted_iota(jnp.int32, (rows, rows), 0) < lax.broadcasted_iota(
            jnp.int32, (rows, rows), 1
        )
        rank = jnp.dot(
            own.astype(F32).astype(BF16),
            before.astype(F32).astype(BF16),
            preferred_element_type=F32,
        )
        slot = jnp.sum(jnp.where(own, rank, 0.0), 0, keepdims=True)
        where = member * cap + slot.astype(jnp.int32)
        place[...] = where
        place_ref[...] = where

    wanted = lax.broadcasted_iota(jnp.int32, (cap, rows), 0) + step * cap
    pick = (wanted == place[...]).astype(F32).astype(BF16)
    out_ref[0] = jnp.dot(pick, hidden[...], preferred_element_type=F32).astype(BF16)


def pack_hidden(ids, gate_column, flat_pre, members, cap):
    rows, both = flat_pre.shape
    width = both // 2
    return pl.pallas_call(
        lambda *refs: pack_kernel(cap, *refs),
        grid=(members,),
        in_specs=[
            pl.BlockSpec((1, rows), lambda q: (0, 0)),
            pl.BlockSpec((rows, 1), lambda q: (0, 0)),
            pl.BlockSpec((rows, both), lambda q: (0, 0)),
        ],
        out_specs=[
            pl.BlockSpec((1, cap, width), lambda q: (q, 0, 0)),
            pl.BlockSpec((1, rows), lambda q: (0, 0)),
        ],
        out_shape=[
            jax.ShapeDtypeStruct((members, cap, width), BF16),
            jax.ShapeDtypeStruct((1, rows), jnp.int32),
        ],
        scratch_shapes=[pltpu.VMEM((rows, width), BF16), pltpu.VMEM((1, rows), jnp.int32)],
        compiler_params=params(),
        cost_estimate=cost(2 * members * cap * rows * width, 2 * rows * both),
    )(ids, gate_column, flat_pre)


def picks(ids, me, cap):
    top, tokens = ids.shape
    experts = [(me ^ mask).astype(F32) for mask in PLANE]
    hits = [(ids == expert).astype(F32) for expert in experts]
    any_hit = hits[0] + hits[1] + hits[2] + hits[3]
    earlier = []
    total = jnp.zeros((1, tokens), F32)
    for k in range(top):
        earlier.append(total)
        total = total + any_hit[k : k + 1]
    before = iota_f32((tokens, tokens), 0) < iota_f32((tokens, tokens), 1)
    base = jnp.dot(
        jnp.broadcast_to(total, (8, tokens)).astype(BF16),
        before.astype(F32).astype(BF16),
        preferred_element_type=F32,
    )[:1]
    rank = base + jnp.concatenate(earlier, 0) + 1.0
    row = iota_f32((cap, tokens), 0) + 1.0
    parts = []
    for hit in hits:
        slot = jnp.sum(hit * rank, 0, keepdims=True)
        parts.append((row == slot).astype(F32).astype(BF16))
    return jnp.concatenate(parts, 1)


def source_ids(block, tokens, top):
    return block[tokens : tokens + ID_ROWS, :tokens].astype(F32)[:top]


def slope_kernel(cap, tokens, top, info, near_ref, far_ref, w0, w1, w2, w3a, w3b, out_ref):
    me = info[0]
    core = me & 1
    near, far = near_ref[...], far_ref[...]
    grads = jnp.concatenate([near[:tokens], far[:tokens]], 0)
    weights = (w0[...], w1[...], w2[...], jnp.concatenate([w3a[...], w3b[...]], 0))
    slopes = [
        lax.dot_general(
            grads, weight, (((1,), (1,)), ((), ())), preferred_element_type=F32
        ).astype(BF16)
        for weight in weights
    ]
    for side, block in enumerate((near, far)):
        pick = picks(source_ids(block, tokens, top), me, cap)
        stacked = jnp.concatenate(
            [slope[side * tokens : (side + 1) * tokens] for slope in slopes], 0
        )
        packed = jnp.dot(pick, stacked, preferred_element_type=F32).astype(BF16)
        out_ref[core if side == 0 else 1 - core] = packed


def packed_slopes(info, near, far, weights, cap, tokens, top):
    block_rows = tokens + ID_ROWS
    blocks = near.shape[0] // block_rows
    model = near.shape[1]
    width = weights[0].shape[0]
    whole = lambda w: pl.BlockSpec(w.shape, lambda j, s: (0, 0))
    return pl.pallas_call(
        lambda *refs: slope_kernel(cap, tokens, top, *refs),
        grid_spec=pltpu.PrefetchScalarGridSpec(
            num_scalar_prefetch=1,
            grid=(blocks,),
            in_specs=[
                pl.BlockSpec((block_rows, model), lambda j, s: (j, 0)),
                pl.BlockSpec((block_rows, model), lambda j, s: (j, 0)),
            ]
            + [whole(w) for w in weights],
            out_specs=pl.BlockSpec((2, cap, width), lambda j, s: (s[1 + j], 0, 0)),
        ),
        out_shape=jax.ShapeDtypeStruct((2 * blocks, cap, width), BF16),
        compiler_params=params(),
        cost_estimate=cost(2 * 2 * blocks * tokens * model * 4 * width, 4 * near.size),
    )(info, near, far, *weights)


def weight_kernel(
    cap, tokens, top, info, near_ref, far_ref, hidden_ref, own_ref, x_ref, y_ref, xk_ref, yk_ref, spread, grads
):
    me = info[0]
    core = me & 1
    block_rows = tokens + ID_ROWS
    blocks = near_ref.shape[0] // block_rows
    width = hidden_ref.shape[2]
    half = width // 2

    def fill(j, carry):
        for side, ref in enumerate((near_ref, far_ref)):
            start = pl.multiple_of(j * block_rows, ID_ROWS)
            block = ref[pl.ds(start, block_rows), :]
            pick = picks(source_ids(block, tokens, top), me, cap)
            member = info[1 + j] * 2 + (core if side == 0 else 1 - core)
            arrived = hidden_ref[member].astype(F32).T.astype(BF16)
            wide = jnp.dot(arrived, pick, preferred_element_type=F32).astype(BF16)
            at = pl.multiple_of((side * blocks + j) * tokens, tokens)
            for e in range(4):
                spread[pl.ds(e * width, width), pl.ds(at, tokens)] = wide[
                    :, e * tokens : (e + 1) * tokens
                ]
            grads[pl.ds(at, tokens), :] = block[:tokens]
        return carry

    lax.fori_loop(0, blocks, fill, 0)

    def product(expert, first, count):
        at = expert * width + first
        return jnp.dot(
            spread[at : at + count, :], grads[...], preferred_element_type=F32
        )

    x_ref[:half] = product(1, 0, half).astype(BF16)
    x_ref[half:] = product(3, 0, half).astype(BF16)
    y_ref[:half] = product(2, half, half).astype(BF16)
    y_ref[half:] = product(3, half, half).astype(BF16)
    own_ref[...] = product(0, 0, width)
    xk_ref[...] = product(1, half, half).astype(BF16)
    yk_ref[...] = product(2, 0, half).astype(BF16)


def weight_partials(info, near, far, hidden, cap, tokens, top):
    blocks = near.shape[0] // (tokens + ID_ROWS)
    model = near.shape[1]
    width = hidden.shape[2]
    half = width // 2
    every = 2 * blocks * tokens
    vmem = pl.BlockSpec(memory_space=pltpu.VMEM)
    return pl.pallas_call(
        lambda *refs: weight_kernel(cap, tokens, top, *refs),
        in_specs=[pl.BlockSpec(memory_space=pltpu.SMEM), vmem, vmem, vmem],
        out_specs=[vmem] * 5,
        out_shape=[
            jax.ShapeDtypeStruct((width, model), F32),
            jax.ShapeDtypeStruct((width, model), BF16),
            jax.ShapeDtypeStruct((width, model), BF16),
            jax.ShapeDtypeStruct((half, model), BF16),
            jax.ShapeDtypeStruct((half, model), BF16),
        ],
        scratch_shapes=[pltpu.VMEM((4 * width, every), BF16), pltpu.VMEM((every, model), BF16)],
        compiler_params=params(0),
        cost_estimate=cost(2 * every * model * 4 * width, 4 * near.size),
    )(info, near, far, hidden)


def finish_kernel(place_ref, gates_ref, pre_ref, back_ref, out_ref):
    rows, both = pre_ref.shape
    width = both // 2
    slots = back_ref.shape[0]
    pick = lax.broadcasted_iota(jnp.int32, (rows, slots), 1) == place_ref[...]
    slope = jnp.dot(
        pick.astype(F32).astype(BF16), back_ref[...], preferred_element_type=F32
    )
    slope = slope * gates_ref[...]
    gate_pre = pre_ref[:, :width].astype(F32)
    up_pre = pre_ref[:, width:].astype(F32)
    sigma = jax.nn.sigmoid(gate_pre)
    out_ref[:, :width] = (
        slope * up_pre * (sigma * (1.0 + gate_pre * (1.0 - sigma)))
    ).astype(BF16)
    out_ref[:, width:] = (slope * (gate_pre * sigma)).astype(BF16)


def finish(place, gate_column, flat_pre, back):
    rows, both = flat_pre.shape
    tile = rows // 4
    return pl.pallas_call(
        finish_kernel,
        grid=(4,),
        in_specs=[
            pl.BlockSpec((tile, 1), lambda i: (i, 0)),
            pl.BlockSpec((tile, 1), lambda i: (i, 0)),
            pl.BlockSpec((tile, both), lambda i: (i, 0)),
            pl.BlockSpec(back.shape, lambda i: (0, 0)),
        ],
        out_specs=pl.BlockSpec((tile, both), lambda i: (i, 0)),
        out_shape=jax.ShapeDtypeStruct((rows, both), BF16),
        compiler_params=params(),
        cost_estimate=cost(2 * rows * both * back.shape[0], 4 * rows * both),
    )(place, gate_column, flat_pre, back)


def per_device(grad_out, gates, expert_ids, pre_acts, w2):
    count = lax.axis_size("expert")
    me = lax.axis_index("expert")
    tokens, top = expert_ids.shape
    model = grad_out.shape[1]
    width = w2.shape[1]
    half = width // 2
    rows = tokens * top
    members = count // 4
    hot = 2 * rows // count
    cold = (rows - 2 * hot) // (count - 2) + 2
    cap = -(-(2 * hot + 2 * cold) // 16) * 16
    groups = [[j for j in range(count) if j & 6 == mask] for mask in PLANE]

    def exchange(chunks):
        return lax.all_to_all(
            chunks, "expert", split_axis=0, concat_axis=0, tiled=True, axis_index_groups=groups
        )

    id_rows = jnp.zeros((ID_ROWS, model), BF16)
    id_rows = lax.dynamic_update_slice(id_rows, expert_ids.T.astype(BF16), (0, 0))
    near = jnp.concatenate([grad_out, id_rows], 0)
    masks = [0]
    bit = count // 2
    while bit >= 8:
        near = jnp.concatenate([near, swap(near, bit)], 0)
        masks = masks + [mask ^ bit for mask in masks]
        bit //= 2

    own_w = lax.all_gather(w2, "dp", axis=2, tiled=True)[0]
    x_w, y_w = swap(own_w, X_BIT), swap(own_w, Y_BIT)
    diag_a, diag_b = swap(x_w[:half], Y_BIT), swap(y_w[half:], X_BIT)
    near, diag_a, diag_b = lax.optimization_barrier((near, diag_a, diag_b))
    far = swap(near, CORE_BIT)
    info = jnp.stack([me] + [(me ^ mask) >> 3 for mask in masks]).astype(jnp.int32)

    flat_pre = pre_acts.reshape(rows, 2 * width)
    gate_column = gates.reshape(rows, 1)
    packed, place = pack_hidden(expert_ids.reshape(1, rows), gate_column, flat_pre, members, cap)
    arrived = exchange(packed)

    slopes = packed_slopes(info, near, far, (own_w, x_w, y_w, diag_a, diag_b), cap, tokens, top)
    back = exchange(slopes).reshape(members * cap, width)

    own, x_send, y_send, x_keep, y_keep = weight_partials(
        info, near, far, arrived, cap, tokens, top
    )
    from_x, from_y = swap(x_send, X_BIT), swap(y_send, Y_BIT)
    to_y = (y_keep.astype(F32) + from_x[half:].astype(F32)).astype(BF16)
    to_x = (x_keep.astype(F32) + from_y[half:].astype(F32)).astype(BF16)
    last_a, last_b = swap(to_y, Y_BIT), swap(to_x, X_BIT)
    total = own + jnp.concatenate(
        [
            from_x[:half].astype(F32) + last_a.astype(F32),
            from_y[:half].astype(F32) + last_b.astype(F32),
        ],
        0,
    )
    total = lax.psum_scatter(total, "dp", scatter_dimension=1, tiled=True)

    pre_grad = finish(place.reshape(rows, 1), gate_column, flat_pre, back)
    return pre_grad.reshape(tokens, top, 2 * width), total[None].astype(BF16)


def solution(mesh):
    in_specs = (
        P(("groups", "expert", "dp"), None),
        P(("groups", "expert", "dp"), None),
        P(("groups", "expert", "dp"), None),
        P(("groups", "expert", "dp"), None, None),
        P("expert", None, "dp"),
    )
    out_specs = (P(("groups", "expert", "dp"), None, None), P("expert", "groups", "dp"))
    return jax.shard_map(
        per_device, mesh=mesh, in_specs=in_specs, out_specs=out_specs, check_vma=False
    )
```

```python
import jax
import jax.numpy as jnp
from jax import lax
from jax.experimental import pallas as pl
from jax.experimental.pallas import tpu as pltpu
from jax.sharding import PartitionSpec as P

X_BIT, Y_BIT, CORE_BIT = 2, 4, 1
PLANE = (0, X_BIT, Y_BIT, X_BIT | Y_BIT)
TAIL = 16
F32, BF16 = jnp.float32, jnp.bfloat16
HIGHEST = lax.Precision.HIGHEST


def params(mebibytes):
    return pltpu.CompilerParams(vmem_limit_bytes=mebibytes * 1024 * 1024)


def cost(flops, moved):
    return pl.CostEstimate(flops=flops, bytes_accessed=moved, transcendentals=0)


def swap(value, bit):
    count = lax.axis_size("expert")
    return lax.ppermute(value, "expert", [(j, j ^ bit) for j in range(count)])


def number(shape, dim):
    return lax.broadcasted_iota(jnp.int32, shape, dim)


def ones_where(condition):
    return condition.astype(F32).astype(BF16)


def dot(a, b):
    return jnp.dot(a, b, preferred_element_type=F32)


def transposed_dot(a, b):
    return lax.dot_general(a, b, (((1,), (1,)), ((), ())), preferred_element_type=F32)


VMEM = pl.BlockSpec(memory_space=pltpu.VMEM)
ANY = pl.BlockSpec(memory_space=pl.ANY)
HBM = pl.BlockSpec(memory_space=pltpu.HBM)
SMEM = pl.BlockSpec(memory_space=pltpu.SMEM)


def pack_kernel(cap, ids_ref, gates_ref, pre_hbm, out_ref, column_ref, pre, sem):
    copy = pltpu.make_async_copy(pre_hbm, pre, sem)
    copy.start()
    members = out_ref.shape[0]
    rows, both = pre.shape
    width = both // 2
    top, tokens = gates_ref.shape
    ids = ids_ref[...]
    member = (ids >> 3) * 2 + (ids & 1)
    hits = jnp.concatenate([(member == q).astype(F32) for q in range(members)], 0)
    size = members * top
    row, col = number((size, size), 0), number((size, size), 1)
    same = row // top == col // top
    earlier = dot(ones_where(same & (col < row)), hits.astype(BF16))
    total = dot(ones_where(same), hits.astype(BF16))
    before = ones_where(number((tokens, tokens), 0) < number((tokens, tokens), 1))
    ranks = hits * (dot(total.astype(BF16), before) + earlier)
    slot = ranks[:top]
    for q in range(1, members):
        slot = slot + ranks[q * top : (q + 1) * top]
    place = member.astype(F32) * cap + slot

    token_of = (number((rows, tokens), 0) // top == number((rows, tokens), 1)).astype(F32)
    wide = lax.dot_general(
        token_of,
        jnp.concatenate([gates_ref[...], place], 0),
        (((1,), (1,)), ((), ())),
        precision=HIGHEST,
        preferred_element_type=F32,
    )
    mine = number((rows, top), 0) % top == number((rows, top), 1)
    gate_column = jnp.sum(jnp.where(mine, wide[:, :top], 0.0), 1, keepdims=True)
    place_column = jnp.sum(jnp.where(mine, wide[:, top:], 0.0), 1, keepdims=True)
    column_ref[...] = jnp.concatenate([gate_column, place_column], 1)
    spread = ones_where(number((tokens, rows), 1) // top == number((tokens, rows), 0))
    labels = jnp.concatenate([slot, member.astype(F32)], 0).astype(BF16)
    wide = dot(labels, spread)
    mine = number((top, rows), 1) % top == number((top, rows), 0)
    slot_line = jnp.sum(jnp.where(mine, wide[:top], 0.0), 0, keepdims=True)
    member_line = jnp.sum(jnp.where(mine, wide[top:], 0.0), 0, keepdims=True)
    place_line = (member_line * cap + slot_line).astype(jnp.int32)

    copy.wait()
    gate_pre = pre[:, :width].astype(F32)
    up_pre = pre[:, width:].astype(F32)
    hidden = (gate_pre * jax.nn.sigmoid(gate_pre) * up_pre * gate_column).astype(BF16)
    line = number((cap, rows), 0)
    tail = number((TAIL, width), 0)
    for q in range(members):
        packed = dot(ones_where(line == place_line - q * cap), hidden)
        first = (q >> 1) * 8 + (q & 1)
        table = [
            jnp.sum(jnp.where(ids == first + mask, slot + 1.0, 0.0), 0, keepdims=True)
            for mask in PLANE
        ]
        rest = jnp.zeros((1, width - tokens), F32)
        upper, lower = jnp.concatenate(table[:3], 1), jnp.concatenate([table[3], rest], 1)
        block = jnp.where(tail == TAIL - 2, upper, jnp.where(tail == TAIL - 1, lower, 0.0))
        out_ref[q, : cap - TAIL] = packed[: cap - TAIL].astype(BF16)
        out_ref[q, cap - TAIL :] = (packed[cap - TAIL :] + block).astype(BF16)


def pack_hidden(ids, gates, flat_pre, members, cap):
    rows, both = flat_pre.shape
    width = both // 2
    return pl.pallas_call(
        lambda *refs: pack_kernel(cap, *refs),
        in_specs=[VMEM, VMEM, HBM],
        out_specs=[VMEM] * 2,
        out_shape=[
            jax.ShapeDtypeStruct((members, cap, width), BF16),
            jax.ShapeDtypeStruct((rows, 2), F32),
        ],
        scratch_shapes=[pltpu.VMEM((rows, both), BF16), pltpu.SemaphoreType.DMA],
        compiler_params=params(60),
        cost_estimate=cost(2 * members * cap * rows * width, 2 * rows * both),
        name="pack_hidden",
    )(ids.T, gates.T, flat_pre)


def picks(chunk, cap, tokens):
    table = chunk[chunk.shape[0] - TAIL :].astype(F32)
    upper, lower = table[TAIL - 2 : TAIL - 1], table[TAIL - 1 :]
    row = (number((cap, tokens), 0) + 1).astype(F32)
    slots = [upper[:, e * tokens : (e + 1) * tokens] for e in range(3)] + [lower[:, :tokens]]
    return slots, row


def pick_for(chunk, me, cap, tokens):
    slots, row = picks(chunk, cap, tokens)
    parts = []
    for mask in PLANE:
        index = ((me ^ mask) >> 1) & 3
        slot = slots[0]
        for e in range(1, 4):
            slot = jnp.where(index == e, slots[e], slot)
        parts.append(ones_where(row == slot))
    return jnp.concatenate(parts, 1)


def gather_copies(sources, target, sem):
    tokens = sources[0].shape[0]
    return [
        pltpu.make_async_copy(ref, target.at[pl.ds(at * tokens, tokens), :], sem.at[at])
        for at, ref in enumerate(sources)
    ]


def place_of(info, at, blocks):
    core = info[0] & 1
    return info[1 + at % blocks] * 2 + (core if at < blocks else 1 - core)


def slope_kernel(cap, count, info, *refs):
    sources, refs = refs[:count], refs[count:]
    w, chunks_ref, out_ref, grads, weights, slopes, chunks, sem, wsem, csem = refs[:7], *refs[7:]
    me = info[0]
    tokens = sources[0].shape[0]
    width = w[0].shape[0]
    half = width // 2
    token_copies = gather_copies(sources, grads, sem)
    starts = (0,) + tuple(width + half * i for i in range(6))
    weight_copies = [
        pltpu.make_async_copy(ref, weights.at[pl.ds(at, ref.shape[0]), :], wsem.at[i])
        for i, (ref, at) in enumerate(zip(w, starts))
    ]
    chunk_copy = pltpu.make_async_copy(chunks_ref.at[:, pl.ds(cap - TAIL, TAIL), :], chunks, csem)
    for copy in token_copies + weight_copies + [chunk_copy]:
        copy.start()
    for copy in token_copies:
        copy.wait()
    for pair in range(2):
        for copy in weight_copies[:3] if pair == 0 else weight_copies[3:]:
            copy.wait()
        two = transposed_dot(
            grads[...], weights[pair * 2 * width : (pair + 1) * 2 * width]
        ).astype(BF16)
        for at in range(count):
            for e in range(2):
                slopes[at, (2 * pair + e) * tokens : (2 * pair + e + 1) * tokens] = two[
                    at * tokens : (at + 1) * tokens, e * width : (e + 1) * width
                ]
    chunk_copy.wait()
    for at in range(count):
        place = place_of(info, at, count // 2)
        pick = pick_for(chunks[place], me, cap, tokens)
        out_ref[place] = dot(pick, slopes[at]).astype(BF16)


def packed_slopes(info, sources, weights, chunks):
    count = len(sources)
    tokens, model = sources[0].shape
    _, cap, width = chunks.shape
    return pl.pallas_call(
        lambda *refs: slope_kernel(cap, count, *refs),
        in_specs=[SMEM] + [ANY] * (count + 8),
        out_specs=VMEM,
        out_shape=jax.ShapeDtypeStruct((count, cap, width), BF16),
        scratch_shapes=[
            pltpu.VMEM((count * tokens, model), BF16),
            pltpu.VMEM((4 * width, model), BF16),
            pltpu.VMEM((count, 4 * tokens, width), BF16),
            pltpu.VMEM((count, TAIL, width), BF16),
            pltpu.SemaphoreType.DMA((count,)),
            pltpu.SemaphoreType.DMA((7,)),
            pltpu.SemaphoreType.DMA,
        ],
        compiler_params=params(60),
        cost_estimate=cost(2 * count * tokens * model * 4 * width, 4 * count * tokens * model),
        name="packed_slopes",
    )(info, *sources, *weights, chunks)


def weight_kernel(cap, count, info, *refs):
    sources, refs = refs[:count], refs[count:]
    hidden, x_send, y_send, own, keep, spread, grads, rows, result, kept, sem, hsem, osem = refs
    me = info[0]
    tokens = sources[0].shape[0]
    width = rows.shape[2]
    half = width // 2
    hidden_copy = pltpu.make_async_copy(hidden, rows, hsem)
    hidden_copy.start()
    token_copies = gather_copies(sources, grads, sem)
    for copy in token_copies:
        copy.start()
    hidden_copy.wait()
    layout = ((2 * width, 2 * width + half), (0, 3 * width), (3 * width + half, width), (half, width + half))
    for at in range(count):
        chunk = rows[place_of(info, at, count // 2)]
        pick = pick_for(chunk, me, cap, tokens)
        wide = dot(chunk.astype(F32).T.astype(BF16), pick).astype(BF16)
        for e in range(4):
            for h in range(2):
                spread[pl.ds(layout[e][h], half), at * tokens : (at + 1) * tokens] = wide[
                    h * half : (h + 1) * half, e * tokens : (e + 1) * tokens
                ]
    for copy in token_copies:
        copy.wait()

    out_copies = []

    def send(source, target):
        copy = pltpu.make_async_copy(source, target, osem.at[len(out_copies)])
        copy.start()
        out_copies.append(copy)

    result[: 2 * width] = dot(spread[: 2 * width], grads[...]).astype(BF16)
    send(result.at[pl.ds(0, width), :], x_send)
    send(result.at[pl.ds(width, width), :], y_send)
    kept[...] = dot(spread[2 * width : 3 * width], grads[...])
    send(kept, own)
    result[2 * width :] = dot(spread[3 * width :], grads[...]).astype(BF16)
    send(result.at[pl.ds(2 * width, width), :], keep)
    for copy in out_copies:
        copy.wait()


def weight_partials(info, sources, hidden):
    count = len(sources)
    tokens, model = sources[0].shape
    _, cap, width = hidden.shape
    every = count * tokens
    return pl.pallas_call(
        lambda *refs: weight_kernel(cap, count, *refs),
        in_specs=[SMEM] + [ANY] * (count + 1),
        out_specs=[ANY] * 4,
        out_shape=[
            jax.ShapeDtypeStruct((width, model), BF16),
            jax.ShapeDtypeStruct((width, model), BF16),
            jax.ShapeDtypeStruct((width, model), F32),
            jax.ShapeDtypeStruct((width, model), BF16),
        ],
        scratch_shapes=[
            pltpu.VMEM((4 * width, every), BF16),
            pltpu.VMEM((every, model), BF16),
            pltpu.VMEM(hidden.shape, BF16),
            pltpu.VMEM((3 * width, model), BF16),
            pltpu.VMEM((width, model), F32),
            pltpu.SemaphoreType.DMA((count,)),
            pltpu.SemaphoreType.DMA,
            pltpu.SemaphoreType.DMA((4,)),
        ],
        compiler_params=params(60),
        cost_estimate=cost(2 * every * model * 4 * width, 4 * every * model),
        name="weight_partials",
    )(info, *sources, hidden)


def finish_kernel(column_ref, pre_ref, back_ref, out_ref):
    rows, both = pre_ref.shape
    width = both // 2
    slots = back_ref.shape[0]
    place = column_ref[:, 1:2].astype(jnp.int32)
    pick = ones_where(number((rows, slots), 1) == place)
    slope = dot(pick, back_ref[...]) * column_ref[:, 0:1]
    gate_pre = pre_ref[:, :width].astype(F32)
    up_pre = pre_ref[:, width:].astype(F32)
    sigma = jax.nn.sigmoid(gate_pre)
    out_ref[:, :width] = (
        slope * up_pre * (sigma * (1.0 + gate_pre * (1.0 - sigma)))
    ).astype(BF16)
    out_ref[:, width:] = (slope * (gate_pre * sigma)).astype(BF16)


def finish(column, flat_pre, back):
    rows, both = flat_pre.shape
    tile = rows // 4
    return pl.pallas_call(
        finish_kernel,
        grid=(4,),
        in_specs=[
            pl.BlockSpec((tile, 2), lambda i: (i, 0)),
            pl.BlockSpec((tile, both), lambda i: (i, 0)),
            pl.BlockSpec(back.shape, lambda i: (0, 0)),
        ],
        out_specs=pl.BlockSpec((tile, both), lambda i: (i, 0)),
        out_shape=jax.ShapeDtypeStruct((rows, both), BF16),
        compiler_params=params(32),
        cost_estimate=cost(rows * both, 4 * rows * both),
        name="finish",
    )(column, flat_pre, back)


def per_device(grad_out, gates, expert_ids, pre_acts, w2):
    count = lax.axis_size("expert")
    me = lax.axis_index("expert")
    tokens, top = expert_ids.shape
    width = w2.shape[1]
    half = width // 2
    rows = tokens * top
    members = count // 4
    hot = 2 * rows // count
    cold = (rows - 2 * hot) // (count - 2) + 2
    cap = -(-(2 * hot + 2 * cold) // 16) * 16
    groups = [[j for j in range(count) if j & 6 == mask] for mask in PLANE]

    def exchange(chunks):
        return lax.all_to_all(
            chunks, "expert", split_axis=0, concat_axis=0, tiled=True, axis_index_groups=groups
        )

    flat_pre = pre_acts.reshape(rows, 2 * width)
    bits = [1 << b for b in reversed(range(3, count.bit_length() - 1))]
    first = [grad_out] + [swap(grad_out, bit) for bit in bits]

    own_w = lax.all_gather(w2, "dp", axis=2, tiled=True)[0]
    upper, lower = own_w[:half], own_w[half:]
    x_a, y_b = swap(upper, X_BIT), swap(lower, Y_BIT)
    diag_a, diag_b = swap(x_a, Y_BIT), swap(y_b, X_BIT)
    x_b, y_a = swap(lower, X_BIT), swap(upper, Y_BIT)

    packed, column = pack_hidden(expert_ids, gates, flat_pre, members, cap)
    masks, path = [0] + bits, {}
    for bit in bits:
        for mask in [m for m in masks if m and not m & bit]:
            masks.append(mask | bit)
            path[mask | bit] = (mask, bit)
    info = jnp.stack([me] + [(me ^ mask) >> 3 for mask in masks]).astype(jnp.int32)

    *first, packed, info = lax.optimization_barrier((*first, packed, info))
    arrived = exchange(packed)
    blocks = dict(zip([0] + bits, first))
    for mask, (known, bit) in path.items():
        blocks[mask] = swap(blocks[known], bit)
    near = list(blocks.values())
    near[-1], x_b, y_a = lax.optimization_barrier((near[-1], x_b, y_a))
    sources = near + [swap(block, CORE_BIT) for block in near]

    x_send, y_send, own, keep = weight_partials(info, sources, arrived)
    slopes = packed_slopes(info, sources, (own_w, x_a, x_b, y_a, y_b, diag_a, diag_b), arrived)
    back = exchange(slopes).reshape(members * cap, width)

    from_x, from_y = swap(x_send, X_BIT), swap(y_send, Y_BIT)
    from_x, from_y = lax.optimization_barrier((from_x, from_y))
    to_y = (keep[half:].astype(F32) + from_x[half:].astype(F32)).astype(BF16)
    to_x = (keep[:half].astype(F32) + from_y[half:].astype(F32)).astype(BF16)
    last_y, last_x = swap(to_y, Y_BIT), swap(to_x, X_BIT)
    total = own + jnp.concatenate(
        [
            from_x[:half].astype(F32) + last_y.astype(F32),
            from_y[:half].astype(F32) + last_x.astype(F32),
        ],
        0,
    )
    total = lax.psum_scatter(total, "dp", scatter_dimension=1, tiled=True)

    pre_grad = finish(column, flat_pre, back)
    return pre_grad.reshape(tokens, top, 2 * width), total[None].astype(BF16)


def solution(mesh):
    in_specs = (
        P(("groups", "expert", "dp"), None),
        P(("groups", "expert", "dp"), None),
        P(("groups", "expert", "dp"), None),
        P(("groups", "expert", "dp"), None, None),
        P("expert", None, "dp"),
    )
    out_specs = (P(("groups", "expert", "dp"), None, None), P("expert", "groups", "dp"))
    return jax.shard_map(
        per_device, mesh=mesh, in_specs=in_specs, out_specs=out_specs, check_vma=False
    )
```

```python
import jax
import jax.numpy as jnp
from jax import lax
from jax.experimental import pallas as pl
from jax.experimental.pallas import tpu as pltpu
from jax.sharding import PartitionSpec as P

X_BIT, Y_BIT, CORE_BIT = 2, 4, 1
PLANE = (0, X_BIT, Y_BIT, X_BIT | Y_BIT)
TAIL = 16
F32, BF16 = jnp.float32, jnp.bfloat16
HIGHEST = lax.Precision.HIGHEST


def params(mebibytes):
    return pltpu.CompilerParams(vmem_limit_bytes=mebibytes * 1024 * 1024)


def cost(flops, moved):
    return pl.CostEstimate(flops=flops, bytes_accessed=moved, transcendentals=0)


def swap(value, bit):
    count = lax.axis_size("expert")
    return lax.ppermute(value, "expert", [(j, j ^ bit) for j in range(count)])


def number(shape, dim):
    return lax.broadcasted_iota(jnp.int32, shape, dim)


def ones_where(condition):
    return condition.astype(F32).astype(BF16)


def dot(a, b):
    return jnp.dot(a, b, preferred_element_type=F32)


def transposed_dot(a, b):
    return lax.dot_general(a, b, (((1,), (1,)), ((), ())), preferred_element_type=F32)


VMEM = pl.BlockSpec(memory_space=pltpu.VMEM)
ANY = pl.BlockSpec(memory_space=pl.ANY)
HBM = pl.BlockSpec(memory_space=pltpu.HBM)
SMEM = pl.BlockSpec(memory_space=pltpu.SMEM)


def spread_line(tokens, rows):
    shift = (rows // tokens).bit_length() - 1
    return ones_where((number((tokens, rows), 1) >> shift) == number((tokens, rows), 0))


def column_of(values, rows):
    top, tokens = values.shape
    shift = top.bit_length() - 1
    high = values.astype(BF16)
    rest = values - high.astype(F32)
    middle = rest.astype(BF16)
    low = (rest - middle.astype(F32)).astype(BF16)
    token_of = ones_where((number((rows, tokens), 0) >> shift) == number((rows, tokens), 1))
    wide = transposed_dot(token_of, jnp.concatenate([high, middle, low], 0))
    wide = wide[:, :top] + (wide[:, top : 2 * top] + wide[:, 2 * top :])
    mine = (number((rows, top), 0) & (top - 1)) == number((rows, top), 1)
    return jnp.sum(jnp.where(mine, wide, 0.0), 1, keepdims=True)


def pack_kernel(cap, ids_ref, gates_ref, pre_hbm, out_ref, place_ref, pre, picks_ref, sem):
    copy = pltpu.make_async_copy(pre_hbm, pre, sem)
    copy.start()
    members = out_ref.shape[0]
    rows, both = pre.shape
    width = both // 2
    top, tokens = gates_ref.shape
    ids = ids_ref[...]
    member = (ids >> 3) * 2 + (ids & 1)
    hits = jnp.concatenate([(member == q).astype(F32) for q in range(members)], 0)
    size = members * top
    shift = top.bit_length() - 1
    row, col = number((size, size), 0), number((size, size), 1)
    same = (row >> shift) == (col >> shift)
    earlier = dot(ones_where(same & (col < row)), hits.astype(BF16))
    total = dot(ones_where(same), hits.astype(BF16))
    before = ones_where(number((tokens, tokens), 0) < number((tokens, tokens), 1))
    ranks = hits * (dot(total.astype(BF16), before) + earlier)
    slot = ranks[:top]
    for q in range(1, members):
        slot = slot + ranks[q * top : (q + 1) * top]
    place = member.astype(F32) * cap + slot

    gate_column = column_of(gates_ref[...], rows)
    wide = dot(jnp.concatenate([slot, member.astype(F32)], 0).astype(BF16), spread_line(tokens, rows))
    mine = (number((top, rows), 1) & (top - 1)) == number((top, rows), 0)
    slot_line = jnp.sum(jnp.where(mine, wide[:top], 0.0), 0, keepdims=True)
    member_line = jnp.sum(jnp.where(mine, wide[top:], 0.0), 0, keepdims=True)
    place_line = (member_line * cap + slot_line).astype(jnp.int32)
    for q in range(members):
        picks_ref[q * cap : (q + 1) * cap] = ones_where(
            number((cap, rows), 0) == place_line - q * cap
        )
    place_ref[...] = jnp.concatenate([slot, member.astype(F32)], 0)

    copy.wait()
    gate_pre = pre[:, :width].astype(F32)
    up_pre = pre[:, width:].astype(F32)
    hidden = (gate_pre * jax.nn.sigmoid(gate_pre) * up_pre * gate_column).astype(BF16)
    every = dot(picks_ref[...], hidden)
    tail = number((TAIL, width), 0)
    for q in range(members):
        packed = every[q * cap : (q + 1) * cap]
        first = (q >> 1) * 8 + (q & 1)
        table = [
            jnp.sum(jnp.where(ids == first + mask, slot + 1.0, 0.0), 0, keepdims=True)
            for mask in PLANE
        ]
        rest = jnp.zeros((1, width - tokens), F32)
        upper, lower = jnp.concatenate(table[:3], 1), jnp.concatenate([table[3], rest], 1)
        block = jnp.where(tail == TAIL - 2, upper, jnp.where(tail == TAIL - 1, lower, 0.0))
        out_ref[q, : cap - TAIL] = packed[: cap - TAIL].astype(BF16)
        out_ref[q, cap - TAIL :] = (packed[cap - TAIL :] + block).astype(BF16)


def pack_hidden(ids, gates, flat_pre, members, cap):
    rows, both = flat_pre.shape
    width = both // 2
    return pl.pallas_call(
        lambda *refs: pack_kernel(cap, *refs),
        in_specs=[VMEM, VMEM, HBM],
        out_specs=[VMEM] * 2,
        out_shape=[
            jax.ShapeDtypeStruct((members, cap, width), BF16),
            jax.ShapeDtypeStruct((2 * gates.shape[1], gates.shape[0]), F32),
        ],
        scratch_shapes=[
            pltpu.VMEM((rows, both), BF16),
            pltpu.VMEM((members * cap, rows), BF16),
            pltpu.SemaphoreType.DMA,
        ],
        compiler_params=params(60),
        cost_estimate=cost(2 * members * cap * rows * width, 2 * rows * both),
        name="pack_hidden",
    )(ids.T, gates.T, flat_pre)


def columns_kernel(cap, place_ref, gates_ref, out_ref):
    top = gates_ref.shape[0]
    rows = out_ref.shape[0]
    place = place_ref[top:] * cap + place_ref[:top]
    out_ref[...] = jnp.concatenate(
        [column_of(gates_ref[...], rows), column_of(place, rows)], 1
    )


def columns(place, gates, cap):
    return pl.pallas_call(
        lambda *refs: columns_kernel(cap, *refs),
        in_specs=[VMEM] * 2,
        out_specs=VMEM,
        out_shape=jax.ShapeDtypeStruct((gates.size, 2), F32),
        compiler_params=params(16),
        name="columns",
    )(place, gates.T)


def picks(chunk, cap, tokens):
    table = chunk[chunk.shape[0] - TAIL :].astype(F32)
    upper, lower = table[TAIL - 2 : TAIL - 1], table[TAIL - 1 :]
    row = (number((cap, tokens), 0) + 1).astype(F32)
    slots = [upper[:, e * tokens : (e + 1) * tokens] for e in range(3)] + [lower[:, :tokens]]
    return slots, row


def pick_for(chunk, me, cap, tokens):
    slots, row = picks(chunk, cap, tokens)
    parts = []
    for mask in PLANE:
        index = ((me ^ mask) >> 1) & 3
        slot = slots[0]
        for e in range(1, 4):
            slot = jnp.where(index == e, slots[e], slot)
        parts.append(ones_where(row == slot))
    return jnp.concatenate(parts, 1)


def gather_copies(sources, target, sem):
    tokens = sources[0].shape[0]
    return [
        pltpu.make_async_copy(ref, target.at[pl.ds(at * tokens, tokens), :], sem.at[at])
        for at, ref in enumerate(sources)
    ]


def place_of(info, at, blocks):
    core = info[0] & 1
    return info[1 + at % blocks] * 2 + (core if at < blocks else 1 - core)


def middle_kernel(cap, count, info, *refs):
    sources, w, refs = refs[:count], refs[count : count + 7], refs[count + 7 :]
    hidden, out_ref, x_diag, y_diag, x_own, y_own, rest, *refs = refs
    grads, weights, rows, spread, pick, slopes, packed, result, sem, wsem, hsem, osem, psem = refs
    me = info[0]
    tokens = sources[0].shape[0]
    width = rows.shape[2]
    half = width // 2
    hidden_copy = pltpu.make_async_copy(hidden, rows, hsem)
    token_copies = gather_copies(sources, grads, sem)
    starts = (0,) + tuple(width + half * i for i in range(6))
    weight_copies = [
        pltpu.make_async_copy(ref, weights.at[pl.ds(at, ref.shape[0]), :], wsem.at[i])
        for i, (ref, at) in enumerate(zip(w, starts))
    ]
    for copy in [hidden_copy] + token_copies + weight_copies:
        copy.start()
    hidden_copy.wait()
    layout = (
        (2 * width, 2 * width + half),
        (width, 3 * width),
        (3 * width + half, width + half),
        (0, half),
    )
    places = [place_of(info, at, count // 2) for at in range(count)]
    for at in range(count):
        chunk = rows[places[at]]
        pick[at] = pick_for(chunk, me, cap, tokens)
        wide = dot(chunk.astype(F32).T.astype(BF16), pick[at]).astype(BF16)
        for e in range(4):
            for h in range(2):
                spread[pl.ds(layout[e][h], half), at * tokens : (at + 1) * tokens] = wide[
                    h * half : (h + 1) * half, e * tokens : (e + 1) * tokens
                ]
    copies = [pltpu.make_async_copy(spread.at[pl.ds(2 * width, 2 * width), :], rest, osem.at[4])]
    copies[0].start()
    for copy in token_copies:
        copy.wait()
    result[...] = dot(spread[: 2 * width], grads[...]).astype(BF16)
    for i, target in enumerate((x_diag, y_diag, x_own, y_own)):
        copy = pltpu.make_async_copy(result.at[pl.ds(i * half, half), :], target, osem.at[i])
        copy.start()
        copies.append(copy)
    for copy in weight_copies:
        copy.wait()
    for first in range(0, count, 2):
        both = transposed_dot(
            grads[first * tokens : (first + 2) * tokens], weights[...]
        ).astype(BF16)
        for at in (first, first + 1):
            side = both[(at - first) * tokens : (at - first + 1) * tokens]
            for e in range(4):
                slopes[at, e * tokens : (e + 1) * tokens] = side[:, e * width : (e + 1) * width]
            packed[at] = dot(pick[at], slopes[at]).astype(BF16)
            copy = pltpu.make_async_copy(packed.at[at], out_ref.at[places[at]], psem.at[at])
            copy.start()
            copies.append(copy)
    for copy in copies:
        copy.wait()


def middle(info, sources, weights, hidden):
    count = len(sources)
    tokens, model = sources[0].shape
    _, cap, width = hidden.shape
    every = count * tokens
    return pl.pallas_call(
        lambda *refs: middle_kernel(cap, count, *refs),
        in_specs=[SMEM] + [ANY] * (count + 8),
        out_specs=[ANY] * 6,
        out_shape=[jax.ShapeDtypeStruct(hidden.shape, BF16)]
        + [jax.ShapeDtypeStruct((width // 2, model), BF16)] * 4
        + [jax.ShapeDtypeStruct((2 * width, every), BF16)],
        scratch_shapes=[
            pltpu.VMEM((every, model), BF16),
            pltpu.VMEM((4 * width, model), BF16),
            pltpu.VMEM(hidden.shape, BF16),
            pltpu.VMEM((4 * width, every), BF16),
            pltpu.VMEM((count, cap, 4 * tokens), BF16),
            pltpu.VMEM((count, 4 * tokens, width), BF16),
            pltpu.VMEM(hidden.shape, BF16),
            pltpu.VMEM((2 * width, model), BF16),
            pltpu.SemaphoreType.DMA((count,)),
            pltpu.SemaphoreType.DMA((7,)),
            pltpu.SemaphoreType.DMA,
            pltpu.SemaphoreType.DMA((5,)),
            pltpu.SemaphoreType.DMA((count,)),
        ],
        compiler_params=params(52),
        cost_estimate=cost(2 * every * model * 6 * width, 4 * every * model),
        name="middle",
    )(info, *sources, *weights, hidden)


def keep_kernel(count, *refs):
    sources, refs = refs[:count], refs[count:]
    rest, own, keep, spread, grads, result, kept, sem, rsem, osem = refs
    width = kept.shape[0]
    rest_copy = pltpu.make_async_copy(rest, spread, rsem)
    copies = [rest_copy] + gather_copies(sources, grads, sem)
    for copy in copies:
        copy.start()
    for copy in copies:
        copy.wait()
    result[...] = dot(spread[width:], grads[...]).astype(BF16)
    keep_copy = pltpu.make_async_copy(result, keep, osem.at[0])
    keep_copy.start()
    kept[...] = dot(spread[:width], grads[...])
    own_copy = pltpu.make_async_copy(kept, own, osem.at[1])
    own_copy.start()
    keep_copy.wait()
    own_copy.wait()


def keep_partials(sources, rest):
    count = len(sources)
    tokens, model = sources[0].shape
    width, every = rest.shape[0] // 2, count * tokens
    return pl.pallas_call(
        lambda *refs: keep_kernel(count, *refs),
        in_specs=[ANY] * (count + 1),
        out_specs=[ANY] * 2,
        out_shape=[
            jax.ShapeDtypeStruct((width, model), F32),
            jax.ShapeDtypeStruct((width, model), BF16),
        ],
        scratch_shapes=[
            pltpu.VMEM((2 * width, every), BF16),
            pltpu.VMEM((every, model), BF16),
            pltpu.VMEM((width, model), BF16),
            pltpu.VMEM((width, model), F32),
            pltpu.SemaphoreType.DMA((count,)),
            pltpu.SemaphoreType.DMA,
            pltpu.SemaphoreType.DMA((2,)),
        ],
        compiler_params=params(52),
        cost_estimate=cost(2 * every * model * 2 * width, 4 * every * model),
        name="keep_partials",
    )(*sources, rest)


def finish_kernel(column_ref, pre_ref, back_ref, out_ref):
    rows, both = pre_ref.shape
    width = both // 2
    slots = back_ref.shape[0]
    place = column_ref[:, 1:2].astype(jnp.int32)
    pick = ones_where(number((rows, slots), 1) == place)
    slope = dot(pick, back_ref[...]) * column_ref[:, 0:1]
    gate_pre = pre_ref[:, :width].astype(F32)
    up_pre = pre_ref[:, width:].astype(F32)
    sigma = jax.nn.sigmoid(gate_pre)
    out_ref[:, :width] = (
        slope * up_pre * (sigma * (1.0 + gate_pre * (1.0 - sigma)))
    ).astype(BF16)
    out_ref[:, width:] = (slope * (gate_pre * sigma)).astype(BF16)


def finish(column, flat_pre, back):
    rows, both = flat_pre.shape
    tile = rows // 4
    return pl.pallas_call(
        finish_kernel,
        grid=(4,),
        in_specs=[
            pl.BlockSpec((tile, 2), lambda i: (i, 0)),
            pl.BlockSpec((tile, both), lambda i: (i, 0)),
            pl.BlockSpec(back.shape, lambda i: (0, 0)),
        ],
        out_specs=pl.BlockSpec((tile, both), lambda i: (i, 0)),
        out_shape=jax.ShapeDtypeStruct((rows, both), BF16),
        compiler_params=params(32),
        cost_estimate=cost(rows * both, 4 * rows * both),
        name="finish",
    )(column, flat_pre, back)


def per_device(grad_out, gates, expert_ids, pre_acts, w2):
    count = lax.axis_size("expert")
    me = lax.axis_index("expert")
    tokens, top = expert_ids.shape
    width = w2.shape[1]
    half = width // 2
    rows = tokens * top
    members = count // 4
    hot = 2 * rows // count
    cold = (rows - 2 * hot) // (count - 2) + 2
    cap = -(-(2 * hot + 2 * cold) // 16) * 16
    groups = [[j for j in range(count) if j & 6 == mask] for mask in PLANE]

    def exchange(chunks):
        return lax.all_to_all(
            chunks, "expert", split_axis=0, concat_axis=0, tiled=True, axis_index_groups=groups
        )

    flat_pre = pre_acts.reshape(rows, 2 * width)
    bits = [1 << b for b in reversed(range(3, count.bit_length() - 1))]
    first = [grad_out] + [swap(grad_out, bit) for bit in bits]

    own_w = lax.all_gather(w2, "dp", axis=2, tiled=True)[0]
    upper, lower = own_w[:half], own_w[half:]
    x_a, y_b = swap(upper, X_BIT), swap(lower, Y_BIT)
    diag_a, diag_b = swap(x_a, Y_BIT), swap(y_b, X_BIT)
    x_b, y_a = swap(lower, X_BIT), swap(upper, Y_BIT)

    packed, place = pack_hidden(expert_ids, gates, flat_pre, members, cap)
    masks, path = [0] + bits, {}
    for bit in bits:
        for mask in [m for m in masks if m > bit and not m & bit and m | bit not in masks]:
            masks.append(mask | bit)
            path[mask | bit] = (mask, bit)
    info = jnp.stack([me] + [(me ^ mask) >> 3 for mask in masks]).astype(jnp.int32)

    *first, packed, info = lax.optimization_barrier((*first, packed, info))
    arrived = exchange(packed)
    blocks = dict(zip([0] + bits, first))
    for mask, (known, bit) in path.items():
        blocks[mask] = swap(blocks[known], bit)
    near = list(blocks.values())
    near[-1], x_b, y_a, diag_a, diag_b = lax.optimization_barrier((near[-1], x_b, y_a, diag_a, diag_b))
    sources = near + [swap(block, CORE_BIT) for block in near]

    slopes, x_diag, y_diag, x_own, y_own, rest = middle(
        info, sources, (own_w, x_a, x_b, y_a, y_b, diag_a, diag_b), arrived
    )
    back = exchange(slopes).reshape(members * cap, width)
    own, keep = keep_partials(sources, rest)

    from_x, from_y = swap(x_diag, X_BIT), swap(y_diag, Y_BIT)
    mine_x, mine_y = swap(x_own, X_BIT), swap(y_own, Y_BIT)
    mine_x, mine_y = lax.optimization_barrier((mine_x, mine_y))
    from_x, from_y = lax.optimization_barrier((from_x, from_y))
    to_y = (keep[half:].astype(F32) + from_x.astype(F32)).astype(BF16)
    to_x = (keep[:half].astype(F32) + from_y.astype(F32)).astype(BF16)
    last_y, last_x = swap(to_y, Y_BIT), swap(to_x, X_BIT)
    total = own + jnp.concatenate(
        [
            mine_x.astype(F32) + last_y.astype(F32),
            mine_y.astype(F32) + last_x.astype(F32),
        ],
        0,
    )
    total = lax.psum_scatter(total, "dp", scatter_dimension=1, tiled=True)

    column = columns(place, gates, cap)
    pre_grad = finish(column, flat_pre, back)
    return pre_grad.reshape(tokens, top, 2 * width), total[None].astype(BF16)


def solution(mesh):
    in_specs = (
        P(("groups", "expert", "dp"), None),
        P(("groups", "expert", "dp"), None),
        P(("groups", "expert", "dp"), None),
        P(("groups", "expert", "dp"), None, None),
        P("expert", None, "dp"),
    )
    out_specs = (P(("groups", "expert", "dp"), None, None), P("expert", "groups", "dp"))
    return jax.shard_map(
        per_device, mesh=mesh, in_specs=in_specs, out_specs=out_specs, check_vma=False
    )
```

```python
import jax
import jax.numpy as jnp
from jax import lax
from jax.experimental import pallas as pl
from jax.experimental.pallas import tpu as pltpu
from jax.sharding import PartitionSpec as P

X_BIT, Y_BIT, CORE_BIT = 2, 4, 1
PLANE = (0, X_BIT, Y_BIT, X_BIT | Y_BIT)
TAIL = 16
F32, BF16 = jnp.float32, jnp.bfloat16
HIGHEST = lax.Precision.HIGHEST


def params(mebibytes):
    return pltpu.CompilerParams(vmem_limit_bytes=mebibytes * 1024 * 1024)


def cost(flops, moved):
    return pl.CostEstimate(flops=flops, bytes_accessed=moved, transcendentals=0)


def swap(value, bit):
    count = lax.axis_size("expert")
    return lax.ppermute(value, "expert", [(j, j ^ bit) for j in range(count)])


def number(shape, dim):
    return lax.broadcasted_iota(jnp.int32, shape, dim)


def ones_where(condition):
    return condition.astype(F32).astype(BF16)


def dot(a, b):
    return jnp.dot(a, b, preferred_element_type=F32)


def transposed_dot(a, b):
    return lax.dot_general(a, b, (((1,), (1,)), ((), ())), preferred_element_type=F32)


VMEM = pl.BlockSpec(memory_space=pltpu.VMEM)
ANY = pl.BlockSpec(memory_space=pl.ANY)
HBM = pl.BlockSpec(memory_space=pltpu.HBM)
SMEM = pl.BlockSpec(memory_space=pltpu.SMEM)


def spread_line(tokens, rows):
    shift = (rows // tokens).bit_length() - 1
    return ones_where((number((tokens, rows), 1) >> shift) == number((tokens, rows), 0))


def column_of(values, rows):
    top, tokens = values.shape
    shift = top.bit_length() - 1
    high = values.astype(BF16)
    rest = values - high.astype(F32)
    middle = rest.astype(BF16)
    low = (rest - middle.astype(F32)).astype(BF16)
    token_of = ones_where((number((rows, tokens), 0) >> shift) == number((rows, tokens), 1))
    wide = transposed_dot(token_of, jnp.concatenate([high, middle, low], 0))
    wide = wide[:, :top] + (wide[:, top : 2 * top] + wide[:, 2 * top :])
    mine = (number((rows, top), 0) & (top - 1)) == number((rows, top), 1)
    return jnp.sum(jnp.where(mine, wide, 0.0), 1, keepdims=True)


def pack_kernel(cap, ids_ref, gates_ref, pre_hbm, out_ref, place_ref, pre, picks_ref, sem):
    copy = pltpu.make_async_copy(pre_hbm, pre, sem)
    copy.start()
    members = out_ref.shape[0]
    rows, both = pre.shape
    width = both // 2
    top, tokens = gates_ref.shape
    ids = ids_ref[...]
    member = (ids >> 3) * 2 + (ids & 1)
    hits = jnp.concatenate([(member == q).astype(F32) for q in range(members)], 0)
    size = members * top
    shift = top.bit_length() - 1
    row, col = number((size, size), 0), number((size, size), 1)
    same = (row >> shift) == (col >> shift)
    earlier = dot(ones_where(same & (col < row)), hits.astype(BF16))
    total = dot(ones_where(same), hits.astype(BF16))
    before = ones_where(number((tokens, tokens), 0) < number((tokens, tokens), 1))
    ranks = hits * (dot(total.astype(BF16), before) + earlier)
    slot = ranks[:top]
    for q in range(1, members):
        slot = slot + ranks[q * top : (q + 1) * top]
    place = member.astype(F32) * cap + slot

    gate_column = column_of(gates_ref[...], rows)
    wide = dot(jnp.concatenate([slot, member.astype(F32)], 0).astype(BF16), spread_line(tokens, rows))
    mine = (number((top, rows), 1) & (top - 1)) == number((top, rows), 0)
    slot_line = jnp.sum(jnp.where(mine, wide[:top], 0.0), 0, keepdims=True)
    member_line = jnp.sum(jnp.where(mine, wide[top:], 0.0), 0, keepdims=True)
    place_line = (member_line * cap + slot_line).astype(jnp.int32)
    for q in range(members):
        picks_ref[q * cap : (q + 1) * cap] = ones_where(
            number((cap, rows), 0) == place_line - q * cap
        )
    place_ref[...] = jnp.concatenate([slot, member.astype(F32)], 0)

    copy.wait()
    gate_pre = pre[:, :width].astype(F32)
    up_pre = pre[:, width:].astype(F32)
    hidden = (gate_pre * jax.nn.sigmoid(gate_pre) * up_pre * gate_column).astype(BF16)
    every = dot(picks_ref[...], hidden)
    tail = number((TAIL, width), 0)
    for q in range(members):
        packed = every[q * cap : (q + 1) * cap]
        first = (q >> 1) * 8 + (q & 1)
        table = [
            jnp.sum(jnp.where(ids == first + mask, slot + 1.0, 0.0), 0, keepdims=True)
            for mask in PLANE
        ]
        rest = jnp.zeros((1, width - tokens), F32)
        upper, lower = jnp.concatenate(table[:3], 1), jnp.concatenate([table[3], rest], 1)
        block = jnp.where(tail == TAIL - 2, upper, jnp.where(tail == TAIL - 1, lower, 0.0))
        out_ref[q, : cap - TAIL] = packed[: cap - TAIL].astype(BF16)
        out_ref[q, cap - TAIL :] = (packed[cap - TAIL :] + block).astype(BF16)


def pack_hidden(ids, gates, flat_pre, members, cap):
    rows, both = flat_pre.shape
    width = both // 2
    return pl.pallas_call(
        lambda *refs: pack_kernel(cap, *refs),
        in_specs=[VMEM, VMEM, HBM],
        out_specs=[VMEM] * 2,
        out_shape=[
            jax.ShapeDtypeStruct((members, cap, width), BF16),
            jax.ShapeDtypeStruct((2 * gates.shape[1], gates.shape[0]), F32),
        ],
        scratch_shapes=[
            pltpu.VMEM((rows, both), BF16),
            pltpu.VMEM((members * cap, rows), BF16),
            pltpu.SemaphoreType.DMA,
        ],
        compiler_params=params(60),
        cost_estimate=cost(2 * members * cap * rows * width, 2 * rows * both),
        name="pack_hidden",
    )(ids.T, gates.T, flat_pre)


def factors_kernel(cap, place_ref, gates_ref, pre_ref, out_ref, column_ref, gate):
    top = gates_ref.shape[0]
    rows = gate.shape[0]
    tile, both = pre_ref.shape
    width = both // 2
    step = pl.program_id(0)

    @pl.when(step == 0)
    def _():
        gate[...] = column_of(gates_ref[...], rows)
        column_ref[...] = column_of(place_ref[top:] * cap + place_ref[:top], rows).astype(jnp.int32)

    gate_pre = pre_ref[:, :width].astype(F32)
    up_pre = pre_ref[:, width:].astype(F32)
    sigma = jax.nn.sigmoid(gate_pre)
    own = gate[pl.ds(pl.multiple_of(step * tile, tile), tile), :]
    out_ref[:, :width] = (own * up_pre * (sigma * (1.0 + gate_pre * (1.0 - sigma)))).astype(BF16)
    out_ref[:, width:] = (own * (gate_pre * sigma)).astype(BF16)


def factors(place, gates, flat_pre, cap):
    rows, both = flat_pre.shape
    tile = rows // 4
    whole = lambda a: pl.BlockSpec(a.shape, lambda i: (0, 0))
    return pl.pallas_call(
        lambda *refs: factors_kernel(cap, *refs),
        grid=(4,),
        in_specs=[whole(place), whole(gates.T), pl.BlockSpec((tile, both), lambda i: (i, 0))],
        out_specs=[
            pl.BlockSpec((tile, both), lambda i: (i, 0)),
            pl.BlockSpec((rows, 1), lambda i: (0, 0)),
        ],
        out_shape=[
            jax.ShapeDtypeStruct((rows, both), BF16),
            jax.ShapeDtypeStruct((rows, 1), jnp.int32),
        ],
        scratch_shapes=[pltpu.VMEM((rows, 1), F32)],
        compiler_params=params(16),
        name="factors",
    )(place, gates.T, flat_pre)


def picks(chunk, cap, tokens):
    table = chunk[chunk.shape[0] - TAIL :].astype(F32)
    upper, lower = table[TAIL - 2 : TAIL - 1], table[TAIL - 1 :]
    row = (number((cap, tokens), 0) + 1).astype(F32)
    slots = [upper[:, e * tokens : (e + 1) * tokens] for e in range(3)] + [lower[:, :tokens]]
    return slots, row


def pick_for(chunk, me, cap, tokens):
    slots, row = picks(chunk, cap, tokens)
    parts = []
    for mask in PLANE:
        index = ((me ^ mask) >> 1) & 3
        slot = slots[0]
        for e in range(1, 4):
            slot = jnp.where(index == e, slots[e], slot)
        parts.append(ones_where(row == slot))
    return jnp.concatenate(parts, 1)


def gather_copies(sources, target, sem):
    tokens = sources[0].shape[0]
    return [
        pltpu.make_async_copy(ref, target.at[pl.ds(at * tokens, tokens), :], sem.at[at])
        for at, ref in enumerate(sources)
    ]


def place_of(info, at, blocks):
    core = info[0] & 1
    return info[1 + at % blocks] * 2 + (core if at < blocks else 1 - core)


def middle_kernel(cap, count, info, *refs):
    sources, w, refs = refs[:count], refs[count : count + 7], refs[count + 7 :]
    hidden, out_ref, x_diag, y_diag, x_own, y_own, rest, *refs = refs
    grads, weights, rows, spread, pick, slopes, packed, result, sem, wsem, hsem, osem, psem = refs
    me = info[0]
    tokens = sources[0].shape[0]
    width = rows.shape[2]
    half = width // 2
    hidden_copy = pltpu.make_async_copy(hidden, rows, hsem)
    token_copies = gather_copies(sources, grads, sem)
    starts = (0,) + tuple(width + half * i for i in range(6))
    weight_copies = [
        pltpu.make_async_copy(ref, weights.at[pl.ds(at, ref.shape[0]), :], wsem.at[i])
        for i, (ref, at) in enumerate(zip(w, starts))
    ]
    for copy in [hidden_copy] + token_copies + weight_copies:
        copy.start()
    hidden_copy.wait()
    layout = (
        (2 * width, 2 * width + half),
        (width, 3 * width),
        (3 * width + half, width + half),
        (0, half),
    )
    places = [place_of(info, at, count // 2) for at in range(count)]
    for at in range(count):
        chunk = rows[places[at]]
        pick[at] = pick_for(chunk, me, cap, tokens)
        wide = dot(chunk.astype(F32).T.astype(BF16), pick[at]).astype(BF16)
        for e in range(4):
            for h in range(2):
                spread[pl.ds(layout[e][h], half), at * tokens : (at + 1) * tokens] = wide[
                    h * half : (h + 1) * half, e * tokens : (e + 1) * tokens
                ]
    copies = [pltpu.make_async_copy(spread.at[pl.ds(2 * width, 2 * width), :], rest, osem.at[4])]
    copies[0].start()
    for copy in token_copies:
        copy.wait()
    result[...] = dot(spread[: 2 * width], grads[...]).astype(BF16)
    for i, target in enumerate((x_diag, y_diag, x_own, y_own)):
        copy = pltpu.make_async_copy(result.at[pl.ds(i * half, half), :], target, osem.at[i])
        copy.start()
        copies.append(copy)
    for copy in weight_copies:
        copy.wait()
    for first in range(0, count, 2):
        both = transposed_dot(
            grads[first * tokens : (first + 2) * tokens], weights[...]
        ).astype(BF16)
        for at in (first, first + 1):
            side = both[(at - first) * tokens : (at - first + 1) * tokens]
            for e in range(4):
                slopes[at, e * tokens : (e + 1) * tokens] = side[:, e * width : (e + 1) * width]
            packed[at] = dot(pick[at], slopes[at]).astype(BF16)
            copy = pltpu.make_async_copy(packed.at[at], out_ref.at[places[at]], psem.at[at])
            copy.start()
            copies.append(copy)
    for copy in copies:
        copy.wait()


def middle(info, sources, weights, hidden):
    count = len(sources)
    tokens, model = sources[0].shape
    _, cap, width = hidden.shape
    every = count * tokens
    return pl.pallas_call(
        lambda *refs: middle_kernel(cap, count, *refs),
        in_specs=[SMEM] + [ANY] * (count + 8),
        out_specs=[ANY] * 6,
        out_shape=[jax.ShapeDtypeStruct(hidden.shape, BF16)]
        + [jax.ShapeDtypeStruct((width // 2, model), BF16)] * 4
        + [jax.ShapeDtypeStruct((2 * width, every), BF16)],
        scratch_shapes=[
            pltpu.VMEM((every, model), BF16),
            pltpu.VMEM((4 * width, model), BF16),
            pltpu.VMEM(hidden.shape, BF16),
            pltpu.VMEM((4 * width, every), BF16),
            pltpu.VMEM((count, cap, 4 * tokens), BF16),
            pltpu.VMEM((count, 4 * tokens, width), BF16),
            pltpu.VMEM(hidden.shape, BF16),
            pltpu.VMEM((2 * width, model), BF16),
            pltpu.SemaphoreType.DMA((count,)),
            pltpu.SemaphoreType.DMA((7,)),
            pltpu.SemaphoreType.DMA,
            pltpu.SemaphoreType.DMA((5,)),
            pltpu.SemaphoreType.DMA((count,)),
        ],
        compiler_params=params(53),
        cost_estimate=cost(2 * every * model * 6 * width, 4 * every * model),
        name="middle",
    )(info, *sources, *weights, hidden)


def keep_kernel(count, *refs):
    sources, refs = refs[:count], refs[count:]
    rest, own, keep, spread, grads, result, kept, sem, rsem, osem = refs
    width = kept.shape[0]
    rest_copy = pltpu.make_async_copy(rest, spread, rsem)
    copies = [rest_copy] + gather_copies(sources, grads, sem)
    for copy in copies:
        copy.start()
    for copy in copies:
        copy.wait()
    result[...] = dot(spread[width:], grads[...]).astype(BF16)
    keep_copy = pltpu.make_async_copy(result, keep, osem.at[0])
    keep_copy.start()
    kept[...] = dot(spread[:width], grads[...])
    own_copy = pltpu.make_async_copy(kept, own, osem.at[1])
    own_copy.start()
    keep_copy.wait()
    own_copy.wait()


def keep_partials(sources, rest):
    count = len(sources)
    tokens, model = sources[0].shape
    width, every = rest.shape[0] // 2, count * tokens
    return pl.pallas_call(
        lambda *refs: keep_kernel(count, *refs),
        in_specs=[ANY] * (count + 1),
        out_specs=[ANY] * 2,
        out_shape=[
            jax.ShapeDtypeStruct((width, model), F32),
            jax.ShapeDtypeStruct((width, model), BF16),
        ],
        scratch_shapes=[
            pltpu.VMEM((2 * width, every), BF16),
            pltpu.VMEM((every, model), BF16),
            pltpu.VMEM((width, model), BF16),
            pltpu.VMEM((width, model), F32),
            pltpu.SemaphoreType.DMA((count,)),
            pltpu.SemaphoreType.DMA,
            pltpu.SemaphoreType.DMA((2,)),
        ],
        compiler_params=params(52),
        cost_estimate=cost(2 * every * model * 2 * width, 4 * every * model),
        name="keep_partials",
    )(*sources, rest)


def finish_kernel(column_ref, factors_ref, back_ref, out_ref):
    rows, both = factors_ref.shape
    width = both // 2
    slots = back_ref.shape[0]
    pick = ones_where(number((rows, slots), 1) == column_ref[...])
    slope = dot(pick, back_ref[...])
    out_ref[:, :width] = (slope * factors_ref[:, :width].astype(F32)).astype(BF16)
    out_ref[:, width:] = (slope * factors_ref[:, width:].astype(F32)).astype(BF16)


def finish(column, scale, back):
    rows, both = scale.shape
    tile = rows // 2
    return pl.pallas_call(
        finish_kernel,
        grid=(2,),
        in_specs=[
            pl.BlockSpec((tile, 1), lambda i: (i, 0)),
            pl.BlockSpec((tile, both), lambda i: (i, 0)),
            pl.BlockSpec(back.shape, lambda i: (0, 0)),
        ],
        out_specs=pl.BlockSpec((tile, both), lambda i: (i, 0)),
        out_shape=jax.ShapeDtypeStruct((rows, both), BF16),
        compiler_params=params(32),
        cost_estimate=cost(rows * both, 4 * rows * both),
        name="finish",
    )(column, scale, back)


def per_device(grad_out, gates, expert_ids, pre_acts, w2):
    count = lax.axis_size("expert")
    me = lax.axis_index("expert")
    tokens, top = expert_ids.shape
    width = w2.shape[1]
    half = width // 2
    rows = tokens * top
    members = count // 4
    hot = 2 * rows // count
    cold = (rows - 2 * hot) // (count - 2) + 2
    cap = -(-(2 * hot + 2 * cold) // 16) * 16
    groups = [[j for j in range(count) if j & 6 == mask] for mask in PLANE]

    def exchange(chunks):
        return lax.all_to_all(
            chunks, "expert", split_axis=0, concat_axis=0, tiled=True, axis_index_groups=groups
        )

    flat_pre = pre_acts.reshape(rows, 2 * width)
    bits = [1 << b for b in reversed(range(3, count.bit_length() - 1))]
    first = [grad_out] + [swap(grad_out, bit) for bit in bits]

    own_w = lax.all_gather(w2, "dp", axis=2, tiled=True)[0]
    upper, lower = own_w[:half], own_w[half:]
    x_a, y_b = swap(upper, X_BIT), swap(lower, Y_BIT)
    diag_a, diag_b = swap(x_a, Y_BIT), swap(y_b, X_BIT)
    x_b, y_a = swap(lower, X_BIT), swap(upper, Y_BIT)

    packed, place = pack_hidden(expert_ids, gates, flat_pre, members, cap)
    masks, path = [0] + bits, {}
    for bit in bits:
        for mask in [m for m in masks if m > bit and not m & bit and m | bit not in masks]:
            masks.append(mask | bit)
            path[mask | bit] = (mask, bit)
    info = jnp.stack([me] + [(me ^ mask) >> 3 for mask in masks]).astype(jnp.int32)

    *first, packed, info = lax.optimization_barrier((*first, packed, info))
    arrived = exchange(packed)
    blocks = dict(zip([0] + bits, first))
    for mask, (known, bit) in path.items():
        blocks[mask] = swap(blocks[known], bit)
    near = list(blocks.values())
    near[-1], x_b, y_a, diag_a, diag_b = lax.optimization_barrier((near[-1], x_b, y_a, diag_a, diag_b))
    sources = near + [swap(block, CORE_BIT) for block in near]

    slopes, x_diag, y_diag, x_own, y_own, rest = middle(
        info, sources, (own_w, x_a, x_b, y_a, y_b, diag_a, diag_b), arrived
    )
    back = exchange(slopes).reshape(members * cap, width)
    own, keep = keep_partials(sources, rest)

    from_x, from_y = swap(x_diag, X_BIT), swap(y_diag, Y_BIT)
    mine_x, mine_y = swap(x_own, X_BIT), swap(y_own, Y_BIT)
    mine_x, mine_y = lax.optimization_barrier((mine_x, mine_y))
    from_x, from_y = lax.optimization_barrier((from_x, from_y))
    to_y = (keep[half:].astype(F32) + from_x.astype(F32)).astype(BF16)
    to_x = (keep[:half].astype(F32) + from_y.astype(F32)).astype(BF16)
    last_y, last_x = swap(to_y, Y_BIT), swap(to_x, X_BIT)
    total = own + jnp.concatenate(
        [
            mine_x.astype(F32) + last_y.astype(F32),
            mine_y.astype(F32) + last_x.astype(F32),
        ],
        0,
    )
    total = lax.psum_scatter(total, "dp", scatter_dimension=1, tiled=True)

    scale, column = factors(place, gates, flat_pre, cap)
    pre_grad = finish(column, scale, back)
    return pre_grad.reshape(tokens, top, 2 * width), total[None].astype(BF16)


def solution(mesh):
    in_specs = (
        P(("groups", "expert", "dp"), None),
        P(("groups", "expert", "dp"), None),
        P(("groups", "expert", "dp"), None),
        P(("groups", "expert", "dp"), None, None),
        P("expert", None, "dp"),
    )
    out_specs = (P(("groups", "expert", "dp"), None, None), P("expert", "groups", "dp"))
    return jax.shard_map(
        per_device, mesh=mesh, in_specs=in_specs, out_specs=out_specs, check_vma=False
    )
```

```python
import jax
import jax.numpy as jnp
from jax import lax
from jax.experimental import pallas as pl
from jax.experimental.pallas import tpu as pltpu
from jax.sharding import PartitionSpec as P

X_BIT, Y_BIT, CORE_BIT = 2, 4, 1
PLANE = (0, X_BIT, Y_BIT, X_BIT | Y_BIT)
TAIL = 16
F32, BF16 = jnp.float32, jnp.bfloat16
HIGHEST = lax.Precision.HIGHEST


def params(mebibytes):
    return pltpu.CompilerParams(vmem_limit_bytes=mebibytes * 1024 * 1024)


def cost(flops, moved):
    return pl.CostEstimate(flops=flops, bytes_accessed=moved, transcendentals=0)


def swap(value, bit):
    count = lax.axis_size("expert")
    return lax.ppermute(value, "expert", [(j, j ^ bit) for j in range(count)])


def number(shape, dim):
    return lax.broadcasted_iota(jnp.int32, shape, dim)


def ones_where(condition):
    return condition.astype(F32).astype(BF16)


def dot(a, b):
    return jnp.dot(a, b, preferred_element_type=F32)


def transposed_dot(a, b):
    return lax.dot_general(a, b, (((1,), (1,)), ((), ())), preferred_element_type=F32)


VMEM = pl.BlockSpec(memory_space=pltpu.VMEM)
ANY = pl.BlockSpec(memory_space=pl.ANY)
HBM = pl.BlockSpec(memory_space=pltpu.HBM)
SMEM = pl.BlockSpec(memory_space=pltpu.SMEM)


def spread_line(tokens, rows):
    shift = (rows // tokens).bit_length() - 1
    return ones_where((number((tokens, rows), 1) >> shift) == number((tokens, rows), 0))


def column_of(values, rows):
    top, tokens = values.shape
    shift = top.bit_length() - 1
    high = values.astype(BF16)
    rest = values - high.astype(F32)
    middle = rest.astype(BF16)
    low = (rest - middle.astype(F32)).astype(BF16)
    token_of = ones_where((number((rows, tokens), 0) >> shift) == number((rows, tokens), 1))
    wide = transposed_dot(token_of, jnp.concatenate([high, middle, low], 0))
    wide = wide[:, :top] + (wide[:, top : 2 * top] + wide[:, 2 * top :])
    mine = (number((rows, top), 0) & (top - 1)) == number((rows, top), 1)
    return jnp.sum(jnp.where(mine, wide, 0.0), 1, keepdims=True)


def pack_kernel(cap, ids_ref, gates_ref, pre_hbm, out_ref, place_ref, pre, picks_ref, sem):
    copy = pltpu.make_async_copy(pre_hbm, pre, sem)
    copy.start()
    members = out_ref.shape[0]
    rows, both = pre.shape
    width = both // 2
    top, tokens = gates_ref.shape
    ids = ids_ref[...]
    member = (ids >> 3) * 2 + (ids & 1)
    hits = jnp.concatenate([(member == q).astype(F32) for q in range(members)], 0)
    size = members * top
    shift = top.bit_length() - 1
    row, col = number((size, size), 0), number((size, size), 1)
    same = (row >> shift) == (col >> shift)
    earlier = dot(ones_where(same & (col < row)), hits.astype(BF16))
    total = dot(ones_where(same), hits.astype(BF16))
    before = ones_where(number((tokens, tokens), 0) < number((tokens, tokens), 1))
    ranks = hits * (dot(total.astype(BF16), before) + earlier)
    slot = ranks[:top]
    for q in range(1, members):
        slot = slot + ranks[q * top : (q + 1) * top]
    place = member.astype(F32) * cap + slot

    gate_column = column_of(gates_ref[...], rows)
    wide = dot(jnp.concatenate([slot, member.astype(F32)], 0).astype(BF16), spread_line(tokens, rows))
    mine = (number((top, rows), 1) & (top - 1)) == number((top, rows), 0)
    slot_line = jnp.sum(jnp.where(mine, wide[:top], 0.0), 0, keepdims=True)
    member_line = jnp.sum(jnp.where(mine, wide[top:], 0.0), 0, keepdims=True)
    place_line = (member_line * cap + slot_line).astype(jnp.int32)
    for q in range(members):
        picks_ref[q * cap : (q + 1) * cap] = ones_where(
            number((cap, rows), 0) == place_line - q * cap
        )
    place_ref[...] = jnp.concatenate([slot, member.astype(F32)], 0)

    copy.wait()
    gate_pre = pre[:, :width].astype(F32)
    up_pre = pre[:, width:].astype(F32)
    hidden = (gate_pre * jax.nn.sigmoid(gate_pre) * up_pre * gate_column).astype(BF16)
    every = dot(picks_ref[...], hidden)
    tail = number((TAIL, width), 0)
    for q in range(members):
        packed = every[q * cap : (q + 1) * cap]
        first = (q >> 1) * 8 + (q & 1)
        table = [
            jnp.sum(jnp.where(ids == first + mask, slot + 1.0, 0.0), 0, keepdims=True)
            for mask in PLANE
        ]
        rest = jnp.zeros((1, width - tokens), F32)
        upper, lower = jnp.concatenate(table[:3], 1), jnp.concatenate([table[3], rest], 1)
        block = jnp.where(tail == TAIL - 2, upper, jnp.where(tail == TAIL - 1, lower, 0.0))
        out_ref[q, : cap - TAIL] = packed[: cap - TAIL].astype(BF16)
        out_ref[q, cap - TAIL :] = (packed[cap - TAIL :] + block).astype(BF16)


def pack_hidden(ids, gates, flat_pre, members, cap):
    rows, both = flat_pre.shape
    width = both // 2
    return pl.pallas_call(
        lambda *refs: pack_kernel(cap, *refs),
        in_specs=[VMEM, VMEM, HBM],
        out_specs=[VMEM] * 2,
        out_shape=[
            jax.ShapeDtypeStruct((members, cap, width), BF16),
            jax.ShapeDtypeStruct((2 * gates.shape[1], gates.shape[0]), F32),
        ],
        scratch_shapes=[
            pltpu.VMEM((rows, both), BF16),
            pltpu.VMEM((members * cap, rows), BF16),
            pltpu.SemaphoreType.DMA,
        ],
        compiler_params=params(60),
        cost_estimate=cost(2 * members * cap * rows * width, 2 * rows * both),
        name="pack_hidden",
    )(ids.T, gates.T, flat_pre)


def factors_kernel(cap, place_ref, gates_ref, pre_ref, out_ref, column_ref, gate):
    top = gates_ref.shape[0]
    rows = gate.shape[0]
    tile, both = pre_ref.shape
    width = both // 2
    step = pl.program_id(0)

    @pl.when(step == 0)
    def _():
        gate[...] = column_of(gates_ref[...], rows)
        column_ref[...] = column_of(place_ref[top:] * cap + place_ref[:top], rows).astype(jnp.int32)

    gate_pre = pre_ref[:, :width].astype(F32)
    up_pre = pre_ref[:, width:].astype(F32)
    sigma = jax.nn.sigmoid(gate_pre)
    own = gate[pl.ds(pl.multiple_of(step * tile, tile), tile), :]
    out_ref[:, :width] = (own * up_pre * (sigma * (1.0 + gate_pre * (1.0 - sigma)))).astype(BF16)
    out_ref[:, width:] = (own * (gate_pre * sigma)).astype(BF16)


def factors(place, gates, flat_pre, cap):
    rows, both = flat_pre.shape
    tile = rows // 4
    whole = lambda a: pl.BlockSpec(a.shape, lambda i: (0, 0))
    return pl.pallas_call(
        lambda *refs: factors_kernel(cap, *refs),
        grid=(4,),
        in_specs=[whole(place), whole(gates.T), pl.BlockSpec((tile, both), lambda i: (i, 0))],
        out_specs=[
            pl.BlockSpec((tile, both), lambda i: (i, 0)),
            pl.BlockSpec((rows, 1), lambda i: (0, 0)),
        ],
        out_shape=[
            jax.ShapeDtypeStruct((rows, both), BF16),
            jax.ShapeDtypeStruct((rows, 1), jnp.int32),
        ],
        scratch_shapes=[pltpu.VMEM((rows, 1), F32)],
        compiler_params=params(16),
        name="factors",
    )(place, gates.T, flat_pre)


def picks(chunk, cap, tokens):
    table = chunk[chunk.shape[0] - TAIL :].astype(F32)
    upper, lower = table[TAIL - 2 : TAIL - 1], table[TAIL - 1 :]
    row = (number((cap, tokens), 0) + 1).astype(F32)
    slots = [upper[:, e * tokens : (e + 1) * tokens] for e in range(3)] + [lower[:, :tokens]]
    return slots, row


def pick_for(chunk, me, cap, tokens):
    slots, row = picks(chunk, cap, tokens)
    parts = []
    for mask in PLANE:
        index = ((me ^ mask) >> 1) & 3
        slot = slots[0]
        for e in range(1, 4):
            slot = jnp.where(index == e, slots[e], slot)
        parts.append(ones_where(row == slot))
    return jnp.concatenate(parts, 1)


def gather_copies(sources, target, sem):
    tokens = sources[0].shape[0]
    return [
        pltpu.make_async_copy(ref, target.at[pl.ds(at * tokens, tokens), :], sem.at[at])
        for at, ref in enumerate(sources)
    ]


def place_of(info, at, blocks):
    core = info[0] & 1
    return info[1 + at % blocks] * 2 + (core if at < blocks else 1 - core)


def middle_kernel(cap, count, info, *refs):
    sources, w, refs = refs[:count], refs[count:-20], refs[-20:]
    hidden, out_ref, x_diag, y_diag, x_own, y_own, rest, *refs = refs
    grads, weights, rows, spread, pick, slopes, packed, result, sem, wsem, hsem, osem, psem = refs
    me = info[0]
    tokens = sources[0].shape[0]
    width = rows.shape[2]
    half = width // 2
    hidden_copy = pltpu.make_async_copy(hidden, rows, hsem)
    token_copies = gather_copies(sources, grads, sem)
    weight_copies, start = [], 0
    for i, ref in enumerate(w):
        weight_copies.append(
            pltpu.make_async_copy(ref, weights.at[pl.ds(start, ref.shape[0]), :], wsem.at[i])
        )
        start += ref.shape[0]
    for copy in [hidden_copy] + token_copies + weight_copies:
        copy.start()
    hidden_copy.wait()
    layout = (
        (2 * width, 2 * width + half),
        (width, 3 * width),
        (3 * width + half, width + half),
        (0, half),
    )
    places = [place_of(info, at, count // 2) for at in range(count)]
    for at in range(count):
        chunk = rows[places[at]]
        pick[at] = pick_for(chunk, me, cap, tokens)
        wide = dot(chunk.astype(F32).T.astype(BF16), pick[at]).astype(BF16)
        for e in range(4):
            for h in range(2):
                spread[pl.ds(layout[e][h], half), at * tokens : (at + 1) * tokens] = wide[
                    h * half : (h + 1) * half, e * tokens : (e + 1) * tokens
                ]
    copies = [pltpu.make_async_copy(spread.at[pl.ds(2 * width, 2 * width), :], rest, osem.at[4])]
    copies[0].start()
    for copy in token_copies:
        copy.wait()
    result[...] = dot(spread[: 2 * width], grads[...]).astype(BF16)
    for i, target in enumerate((x_diag, y_diag, x_own, y_own)):
        copy = pltpu.make_async_copy(result.at[pl.ds(i * half, half), :], target, osem.at[i])
        copy.start()
        copies.append(copy)
    for copy in weight_copies:
        copy.wait()
    for first in range(0, count, 2):
        both = transposed_dot(
            grads[first * tokens : (first + 2) * tokens], weights[...]
        ).astype(BF16)
        for at in (first, first + 1):
            side = both[(at - first) * tokens : (at - first + 1) * tokens]
            for e in range(4):
                slopes[at, e * tokens : (e + 1) * tokens] = side[:, e * width : (e + 1) * width]
            packed[at] = dot(pick[at], slopes[at]).astype(BF16)
            copy = pltpu.make_async_copy(packed.at[at], out_ref.at[places[at]], psem.at[at])
            copy.start()
            copies.append(copy)
    for copy in copies:
        copy.wait()


def middle(info, sources, weights, hidden):
    count = len(sources)
    tokens, model = sources[0].shape
    _, cap, width = hidden.shape
    every = count * tokens
    return pl.pallas_call(
        lambda *refs: middle_kernel(cap, count, *refs),
        in_specs=[SMEM] + [ANY] * (count + len(weights) + 1),
        out_specs=[ANY] * 6,
        out_shape=[jax.ShapeDtypeStruct(hidden.shape, BF16)]
        + [jax.ShapeDtypeStruct((width // 2, model), BF16)] * 4
        + [jax.ShapeDtypeStruct((2 * width, every), BF16)],
        scratch_shapes=[
            pltpu.VMEM((every, model), BF16),
            pltpu.VMEM((4 * width, model), BF16),
            pltpu.VMEM(hidden.shape, BF16),
            pltpu.VMEM((4 * width, every), BF16),
            pltpu.VMEM((count, cap, 4 * tokens), BF16),
            pltpu.VMEM((count, 4 * tokens, width), BF16),
            pltpu.VMEM(hidden.shape, BF16),
            pltpu.VMEM((2 * width, model), BF16),
            pltpu.SemaphoreType.DMA((count,)),
            pltpu.SemaphoreType.DMA((len(weights),)),
            pltpu.SemaphoreType.DMA,
            pltpu.SemaphoreType.DMA((5,)),
            pltpu.SemaphoreType.DMA((count,)),
        ],
        compiler_params=params(52),
        cost_estimate=cost(2 * every * model * 6 * width, 4 * every * model),
        name="middle",
    )(info, *sources, *weights, hidden)


def keep_kernel(count, *refs):
    sources, refs = refs[:count], refs[count:]
    rest, own, keep, spread, grads, result, kept, sem, rsem, osem = refs
    width = kept.shape[0]
    rest_copy = pltpu.make_async_copy(rest, spread, rsem)
    copies = [rest_copy] + gather_copies(sources, grads, sem)
    for copy in copies:
        copy.start()
    for copy in copies:
        copy.wait()
    result[...] = dot(spread[width:], grads[...]).astype(BF16)
    keep_copy = pltpu.make_async_copy(result, keep, osem.at[0])
    keep_copy.start()
    kept[...] = dot(spread[:width], grads[...])
    own_copy = pltpu.make_async_copy(kept, own, osem.at[1])
    own_copy.start()
    keep_copy.wait()
    own_copy.wait()


def keep_partials(sources, rest):
    count = len(sources)
    tokens, model = sources[0].shape
    width, every = rest.shape[0] // 2, count * tokens
    return pl.pallas_call(
        lambda *refs: keep_kernel(count, *refs),
        in_specs=[ANY] * (count + 1),
        out_specs=[ANY] * 2,
        out_shape=[
            jax.ShapeDtypeStruct((width, model), F32),
            jax.ShapeDtypeStruct((width, model), BF16),
        ],
        scratch_shapes=[
            pltpu.VMEM((2 * width, every), BF16),
            pltpu.VMEM((every, model), BF16),
            pltpu.VMEM((width, model), BF16),
            pltpu.VMEM((width, model), F32),
            pltpu.SemaphoreType.DMA((count,)),
            pltpu.SemaphoreType.DMA,
            pltpu.SemaphoreType.DMA((2,)),
        ],
        compiler_params=params(52),
        cost_estimate=cost(2 * every * model * 2 * width, 4 * every * model),
        name="keep_partials",
    )(*sources, rest)


def finish_kernel(column_ref, factors_ref, back_ref, out_ref):
    rows, both = factors_ref.shape
    width = both // 2
    slots = back_ref.shape[0]
    pick = ones_where(number((rows, slots), 1) == column_ref[...])
    slope = dot(pick, back_ref[...])
    out_ref[:, :width] = (slope * factors_ref[:, :width].astype(F32)).astype(BF16)
    out_ref[:, width:] = (slope * factors_ref[:, width:].astype(F32)).astype(BF16)


def finish(column, scale, back):
    rows, both = scale.shape
    tile = rows // 2
    return pl.pallas_call(
        finish_kernel,
        grid=(2,),
        in_specs=[
            pl.BlockSpec((tile, 1), lambda i: (i, 0)),
            pl.BlockSpec((tile, both), lambda i: (i, 0)),
            pl.BlockSpec(back.shape, lambda i: (0, 0)),
        ],
        out_specs=pl.BlockSpec((tile, both), lambda i: (i, 0)),
        out_shape=jax.ShapeDtypeStruct((rows, both), BF16),
        compiler_params=params(32),
        cost_estimate=cost(rows * both, 4 * rows * both),
        name="finish",
    )(column, scale, back)


def per_device(grad_out, gates, expert_ids, pre_acts, w2):
    count = lax.axis_size("expert")
    me = lax.axis_index("expert")
    tokens, top = expert_ids.shape
    width = w2.shape[1]
    half = width // 2
    rows = tokens * top
    members = count // 4
    hot = 2 * rows // count
    cold = (rows - 2 * hot) // (count - 2) + 2
    cap = -(-(2 * hot + 2 * cold) // 16) * 16
    groups = [[j for j in range(count) if j & 6 == mask] for mask in PLANE]

    def exchange(chunks):
        return lax.all_to_all(
            chunks, "expert", split_axis=0, concat_axis=0, tiled=True, axis_index_groups=groups
        )

    flat_pre = pre_acts.reshape(rows, 2 * width)
    bits = [1 << b for b in reversed(range(3, count.bit_length() - 1))]
    first = [grad_out] + [swap(grad_out, bit) for bit in bits]

    own_w = lax.all_gather(w2, "dp", axis=2, tiled=True)[0]
    quarter = half // 2
    x_a1, y_b1 = swap(own_w[:quarter], X_BIT), swap(own_w[half : half + quarter], Y_BIT)
    x_a2, y_b2 = swap(own_w[quarter:half], X_BIT), swap(own_w[half + quarter :], Y_BIT)
    diag = [
        swap(jnp.concatenate([x_a1, x_a2], 0), Y_BIT),
        swap(jnp.concatenate([y_b1, y_b2], 0), X_BIT),
    ]
    x_b, y_a = swap(own_w[half:], X_BIT), swap(own_w[:half], Y_BIT)

    packed, place = pack_hidden(expert_ids, gates, flat_pre, members, cap)
    masks, path = [0] + bits, {}
    for bit in bits:
        for mask in [m for m in masks if m > bit and not m & bit and m | bit not in masks]:
            masks.append(mask | bit)
            path[mask | bit] = (mask, bit)
    info = jnp.stack([me] + [(me ^ mask) >> 3 for mask in masks]).astype(jnp.int32)

    *first, x_a1, y_b1, packed, info = lax.optimization_barrier((*first, x_a1, y_b1, packed, info))
    arrived = exchange(packed)
    blocks = dict(zip([0] + bits, first))
    for mask, (known, bit) in path.items():
        blocks[mask] = swap(blocks[known], bit)
    near = list(blocks.values())
    near[-1], x_b, y_a, *diag = lax.optimization_barrier((near[-1], x_b, y_a, *diag))
    sources = near + [swap(block, CORE_BIT) for block in near]

    slopes, x_diag, y_diag, x_own, y_own, rest = middle(
        info, sources, (own_w, x_a1, x_a2, x_b, y_a, y_b1, y_b2, *diag), arrived
    )
    back = exchange(slopes).reshape(members * cap, width)
    own, keep = keep_partials(sources, rest)

    from_x, from_y = swap(x_diag, X_BIT), swap(y_diag, Y_BIT)
    mine_x, mine_y = swap(x_own, X_BIT), swap(y_own, Y_BIT)
    mine_x, mine_y = lax.optimization_barrier((mine_x, mine_y))
    from_x, from_y = lax.optimization_barrier((from_x, from_y))
    to_y = (keep[half:].astype(F32) + from_x.astype(F32)).astype(BF16)
    to_x = (keep[:half].astype(F32) + from_y.astype(F32)).astype(BF16)
    last_y, last_x = swap(to_y, Y_BIT), swap(to_x, X_BIT)
    total = own + jnp.concatenate(
        [
            mine_x.astype(F32) + last_y.astype(F32),
            mine_y.astype(F32) + last_x.astype(F32),
        ],
        0,
    )
    total = lax.psum_scatter(total, "dp", scatter_dimension=1, tiled=True)

    scale, column = factors(place, gates, flat_pre, cap)
    pre_grad = finish(column, scale, back)
    return pre_grad.reshape(tokens, top, 2 * width), total[None].astype(BF16)


def solution(mesh):
    in_specs = (
        P(("groups", "expert", "dp"), None),
        P(("groups", "expert", "dp"), None),
        P(("groups", "expert", "dp"), None),
        P(("groups", "expert", "dp"), None, None),
        P("expert", None, "dp"),
    )
    out_specs = (P(("groups", "expert", "dp"), None, None), P("expert", "groups", "dp"))
    return jax.shard_map(
        per_device, mesh=mesh, in_specs=in_specs, out_specs=out_specs, check_vma=False
    )
```

```python
import jax
import jax.numpy as jnp
from jax import lax
from jax.experimental import pallas as pl
from jax.experimental.pallas import tpu as pltpu
from jax.sharding import PartitionSpec as P

X_BIT, Y_BIT, CORE_BIT = 2, 4, 1
PLANE = (0, X_BIT, Y_BIT, X_BIT | Y_BIT)
TAIL = 16
F32, BF16 = jnp.float32, jnp.bfloat16
HIGHEST = lax.Precision.HIGHEST


def params(mebibytes):
    return pltpu.CompilerParams(vmem_limit_bytes=mebibytes * 1024 * 1024)


def cost(flops, moved):
    return pl.CostEstimate(flops=flops, bytes_accessed=moved, transcendentals=0)


def swap(value, bit):
    count = lax.axis_size("expert")
    return lax.ppermute(value, "expert", [(j, j ^ bit) for j in range(count)])


def number(shape, dim):
    return lax.broadcasted_iota(jnp.int32, shape, dim)


def ones_where(condition):
    return condition.astype(F32).astype(BF16)


def dot(a, b):
    return jnp.dot(a, b, preferred_element_type=F32)


def transposed_dot(a, b):
    return lax.dot_general(a, b, (((1,), (1,)), ((), ())), preferred_element_type=F32)


VMEM = pl.BlockSpec(memory_space=pltpu.VMEM)
ANY = pl.BlockSpec(memory_space=pl.ANY)
HBM = pl.BlockSpec(memory_space=pltpu.HBM)
SMEM = pl.BlockSpec(memory_space=pltpu.SMEM)


def spread_line(tokens, rows):
    shift = (rows // tokens).bit_length() - 1
    return ones_where((number((tokens, rows), 1) >> shift) == number((tokens, rows), 0))


def column_of(values, rows):
    top, tokens = values.shape
    shift = top.bit_length() - 1
    high = values.astype(BF16)
    rest = values - high.astype(F32)
    middle = rest.astype(BF16)
    low = (rest - middle.astype(F32)).astype(BF16)
    token_of = ones_where((number((rows, tokens), 0) >> shift) == number((rows, tokens), 1))
    wide = transposed_dot(token_of, jnp.concatenate([high, middle, low], 0))
    wide = wide[:, :top] + (wide[:, top : 2 * top] + wide[:, 2 * top :])
    mine = (number((rows, top), 0) & (top - 1)) == number((rows, top), 1)
    return jnp.sum(jnp.where(mine, wide, 0.0), 1, keepdims=True)


def pack_kernel(cap, ids_ref, gates_ref, pre_hbm, out_ref, place_ref, pre, picks_ref, sem):
    copy = pltpu.make_async_copy(pre_hbm, pre, sem)
    copy.start()
    members = out_ref.shape[0]
    rows, both = pre.shape
    width = both // 2
    top, tokens = gates_ref.shape
    ids = ids_ref[...]
    member = (ids >> 3) * 2 + (ids & 1)
    hits = jnp.concatenate([(member == q).astype(F32) for q in range(members)], 0)
    size = members * top
    shift = top.bit_length() - 1
    row, col = number((size, size), 0), number((size, size), 1)
    same = (row >> shift) == (col >> shift)
    earlier = dot(ones_where(same & (col < row)), hits.astype(BF16))
    total = dot(ones_where(same), hits.astype(BF16))
    before = ones_where(number((tokens, tokens), 0) < number((tokens, tokens), 1))
    ranks = hits * (dot(total.astype(BF16), before) + earlier)
    slot = ranks[:top]
    for q in range(1, members):
        slot = slot + ranks[q * top : (q + 1) * top]
    place = member.astype(F32) * cap + slot

    gate_column = column_of(gates_ref[...], rows)
    wide = dot(jnp.concatenate([slot, member.astype(F32)], 0).astype(BF16), spread_line(tokens, rows))
    mine = (number((top, rows), 1) & (top - 1)) == number((top, rows), 0)
    slot_line = jnp.sum(jnp.where(mine, wide[:top], 0.0), 0, keepdims=True)
    member_line = jnp.sum(jnp.where(mine, wide[top:], 0.0), 0, keepdims=True)
    place_line = (member_line * cap + slot_line).astype(jnp.int32)
    for q in range(members):
        picks_ref[q * cap : (q + 1) * cap] = ones_where(
            number((cap, rows), 0) == place_line - q * cap
        )
    place_ref[...] = jnp.concatenate([slot, member.astype(F32)], 0)

    copy.wait()
    gate_pre = pre[:, :width].astype(F32)
    up_pre = pre[:, width:].astype(F32)
    hidden = (gate_pre * jax.nn.sigmoid(gate_pre) * up_pre * gate_column).astype(BF16)
    every = dot(picks_ref[...], hidden)
    tail = number((TAIL, width), 0)
    for q in range(members):
        packed = every[q * cap : (q + 1) * cap]
        first = (q >> 1) * 8 + (q & 1)
        table = [
            jnp.sum(jnp.where(ids == first + mask, slot + 1.0, 0.0), 0, keepdims=True)
            for mask in PLANE
        ]
        rest = jnp.zeros((1, width - tokens), F32)
        upper, lower = jnp.concatenate(table[:3], 1), jnp.concatenate([table[3], rest], 1)
        block = jnp.where(tail == TAIL - 2, upper, jnp.where(tail == TAIL - 1, lower, 0.0))
        out_ref[q, : cap - TAIL] = packed[: cap - TAIL].astype(BF16)
        out_ref[q, cap - TAIL :] = (packed[cap - TAIL :] + block).astype(BF16)


def pack_hidden(ids, gates, flat_pre, members, cap):
    rows, both = flat_pre.shape
    width = both // 2
    return pl.pallas_call(
        lambda *refs: pack_kernel(cap, *refs),
        in_specs=[VMEM, VMEM, HBM],
        out_specs=[VMEM] * 2,
        out_shape=[
            jax.ShapeDtypeStruct((members, cap, width), BF16),
            jax.ShapeDtypeStruct((2 * gates.shape[1], gates.shape[0]), F32),
        ],
        scratch_shapes=[
            pltpu.VMEM((rows, both), BF16),
            pltpu.VMEM((members * cap, rows), BF16),
            pltpu.SemaphoreType.DMA,
        ],
        compiler_params=params(60),
        cost_estimate=cost(2 * members * cap * rows * width, 2 * rows * both),
        name="pack_hidden",
    )(ids.T, gates.T, flat_pre)


def factors_kernel(cap, place_ref, gates_ref, pre_ref, out_ref, column_ref, gate):
    top = gates_ref.shape[0]
    rows = gate.shape[0]
    tile, both = pre_ref.shape
    width = both // 2
    step = pl.program_id(0)

    @pl.when(step == 0)
    def _():
        gate[...] = column_of(gates_ref[...], rows)
        column_ref[...] = column_of(place_ref[top:] * cap + place_ref[:top], rows).astype(jnp.int32)

    gate_pre = pre_ref[:, :width].astype(F32)
    up_pre = pre_ref[:, width:].astype(F32)
    sigma = jax.nn.sigmoid(gate_pre)
    own = gate[pl.ds(pl.multiple_of(step * tile, tile), tile), :]
    out_ref[:, :width] = (own * up_pre * (sigma * (1.0 + gate_pre * (1.0 - sigma)))).astype(BF16)
    out_ref[:, width:] = (own * (gate_pre * sigma)).astype(BF16)


def factors(place, gates, flat_pre, cap):
    rows, both = flat_pre.shape
    tile = rows // 4
    whole = lambda a: pl.BlockSpec(a.shape, lambda i: (0, 0))
    return pl.pallas_call(
        lambda *refs: factors_kernel(cap, *refs),
        grid=(4,),
        in_specs=[whole(place), whole(gates.T), pl.BlockSpec((tile, both), lambda i: (i, 0))],
        out_specs=[
            pl.BlockSpec((tile, both), lambda i: (i, 0)),
            pl.BlockSpec((rows, 1), lambda i: (0, 0)),
        ],
        out_shape=[
            jax.ShapeDtypeStruct((rows, both), BF16),
            jax.ShapeDtypeStruct((rows, 1), jnp.int32),
        ],
        scratch_shapes=[pltpu.VMEM((rows, 1), F32)],
        compiler_params=params(16),
        name="factors",
    )(place, gates.T, flat_pre)


def picks(chunk, cap, tokens):
    table = chunk[chunk.shape[0] - TAIL :].astype(F32)
    upper, lower = table[TAIL - 2 : TAIL - 1], table[TAIL - 1 :]
    row = (number((cap, tokens), 0) + 1).astype(F32)
    slots = [upper[:, e * tokens : (e + 1) * tokens] for e in range(3)] + [lower[:, :tokens]]
    return slots, row


def pick_for(chunk, me, cap, tokens):
    slots, row = picks(chunk, cap, tokens)
    parts = []
    for mask in PLANE:
        index = ((me ^ mask) >> 1) & 3
        slot = slots[0]
        for e in range(1, 4):
            slot = jnp.where(index == e, slots[e], slot)
        parts.append(ones_where(row == slot))
    return jnp.concatenate(parts, 1)


def gather_copies(sources, target, sem):
    tokens = sources[0].shape[0]
    return [
        pltpu.make_async_copy(ref, target.at[pl.ds(at * tokens, tokens), :], sem.at[at])
        for at, ref in enumerate(sources)
    ]


def place_of(info, at, blocks):
    core = info[0] & 1
    return info[1 + at % blocks] * 2 + (core if at < blocks else 1 - core)


def middle_kernel(cap, count, info, *refs):
    sources, w, refs = refs[:count], refs[count:-20], refs[-20:]
    hidden, out_ref, x_diag, y_diag, x_own, y_own, rest, *refs = refs
    grads, weights, rows, spread, pick, slopes, packed, result, sem, wsem, hsem, osem, psem = refs
    me = info[0]
    tokens = sources[0].shape[0]
    width = rows.shape[2]
    half = width // 2
    hidden_copy = pltpu.make_async_copy(hidden, rows, hsem)
    token_copies = gather_copies(sources, grads, sem)
    weight_copies, start = [], 0
    for i, ref in enumerate(w):
        weight_copies.append(
            pltpu.make_async_copy(ref, weights.at[pl.ds(start, ref.shape[0]), :], wsem.at[i])
        )
        start += ref.shape[0]
    for copy in [hidden_copy] + token_copies + weight_copies:
        copy.start()
    hidden_copy.wait()
    layout = (
        (2 * width, 2 * width + half),
        (width, 3 * width),
        (3 * width + half, width + half),
        (0, half),
    )
    places = [place_of(info, at, count // 2) for at in range(count)]
    for at in range(count):
        chunk = rows[places[at]]
        pick[at] = pick_for(chunk, me, cap, tokens)
        wide = dot(chunk.astype(F32).T.astype(BF16), pick[at]).astype(BF16)
        for e in range(4):
            for h in range(2):
                spread[pl.ds(layout[e][h], half), at * tokens : (at + 1) * tokens] = wide[
                    h * half : (h + 1) * half, e * tokens : (e + 1) * tokens
                ]
    copies = [pltpu.make_async_copy(spread.at[pl.ds(2 * width, 2 * width), :], rest, osem.at[4])]
    copies[0].start()
    for copy in token_copies:
        copy.wait()
    result[...] = dot(spread[: 2 * width], grads[...]).astype(BF16)
    for i, target in enumerate((x_diag, y_diag, x_own, y_own)):
        copy = pltpu.make_async_copy(result.at[pl.ds(i * half, half), :], target, osem.at[i])
        copy.start()
        copies.append(copy)
    for copy in weight_copies:
        copy.wait()
    for first in range(0, count, 4):
        four = transposed_dot(
            grads[first * tokens : (first + 4) * tokens], weights[...]
        ).astype(BF16)
        for at in range(first, first + 4):
            side = four[(at - first) * tokens : (at - first + 1) * tokens]
            for e in range(4):
                slopes[at, e * tokens : (e + 1) * tokens] = side[:, e * width : (e + 1) * width]
            packed[at] = dot(pick[at], slopes[at]).astype(BF16)
        for at in range(first, first + 4):
            copy = pltpu.make_async_copy(packed.at[at], out_ref.at[places[at]], psem.at[at])
            copy.start()
            copies.append(copy)
    for copy in copies:
        copy.wait()


def middle(info, sources, weights, hidden):
    count = len(sources)
    tokens, model = sources[0].shape
    _, cap, width = hidden.shape
    every = count * tokens
    return pl.pallas_call(
        lambda *refs: middle_kernel(cap, count, *refs),
        in_specs=[SMEM] + [ANY] * (count + len(weights) + 1),
        out_specs=[ANY] * 6,
        out_shape=[jax.ShapeDtypeStruct(hidden.shape, BF16)]
        + [jax.ShapeDtypeStruct((width // 2, model), BF16)] * 4
        + [jax.ShapeDtypeStruct((2 * width, every), BF16)],
        scratch_shapes=[
            pltpu.VMEM((every, model), BF16),
            pltpu.VMEM((4 * width, model), BF16),
            pltpu.VMEM(hidden.shape, BF16),
            pltpu.VMEM((4 * width, every), BF16),
            pltpu.VMEM((count, cap, 4 * tokens), BF16),
            pltpu.VMEM((count, 4 * tokens, width), BF16),
            pltpu.VMEM(hidden.shape, BF16),
            pltpu.VMEM((2 * width, model), BF16),
            pltpu.SemaphoreType.DMA((count,)),
            pltpu.SemaphoreType.DMA((len(weights),)),
            pltpu.SemaphoreType.DMA,
            pltpu.SemaphoreType.DMA((5,)),
            pltpu.SemaphoreType.DMA((count,)),
        ],
        compiler_params=params(52),
        cost_estimate=cost(2 * every * model * 6 * width, 4 * every * model),
        name="middle",
    )(info, *sources, *weights, hidden)


def keep_kernel(count, *refs):
    sources, refs = refs[:count], refs[count:]
    rest, own, keep, spread, grads, result, kept, sem, rsem, osem = refs
    width = kept.shape[0]
    rest_copy = pltpu.make_async_copy(rest, spread, rsem)
    copies = [rest_copy] + gather_copies(sources, grads, sem)
    for copy in copies:
        copy.start()
    for copy in copies:
        copy.wait()
    result[...] = dot(spread[width:], grads[...]).astype(BF16)
    keep_copy = pltpu.make_async_copy(result, keep, osem.at[0])
    keep_copy.start()
    kept[...] = dot(spread[:width], grads[...])
    own_copy = pltpu.make_async_copy(kept, own, osem.at[1])
    own_copy.start()
    keep_copy.wait()
    own_copy.wait()


def keep_partials(sources, rest):
    count = len(sources)
    tokens, model = sources[0].shape
    width, every = rest.shape[0] // 2, count * tokens
    return pl.pallas_call(
        lambda *refs: keep_kernel(count, *refs),
        in_specs=[ANY] * (count + 1),
        out_specs=[ANY] * 2,
        out_shape=[
            jax.ShapeDtypeStruct((width, model), F32),
            jax.ShapeDtypeStruct((width, model), BF16),
        ],
        scratch_shapes=[
            pltpu.VMEM((2 * width, every), BF16),
            pltpu.VMEM((every, model), BF16),
            pltpu.VMEM((width, model), BF16),
            pltpu.VMEM((width, model), F32),
            pltpu.SemaphoreType.DMA((count,)),
            pltpu.SemaphoreType.DMA,
            pltpu.SemaphoreType.DMA((2,)),
        ],
        compiler_params=params(52),
        cost_estimate=cost(2 * every * model * 2 * width, 4 * every * model),
        name="keep_partials",
    )(*sources, rest)


def finish_kernel(column_ref, factors_ref, back_ref, out_ref):
    rows, both = factors_ref.shape
    width = both // 2
    slots = back_ref.shape[0]
    pick = ones_where(number((rows, slots), 1) == column_ref[...])
    slope = dot(pick, back_ref[...])
    out_ref[:, :width] = (slope * factors_ref[:, :width].astype(F32)).astype(BF16)
    out_ref[:, width:] = (slope * factors_ref[:, width:].astype(F32)).astype(BF16)


def finish(column, scale, back):
    rows, both = scale.shape
    tile = rows // 2
    return pl.pallas_call(
        finish_kernel,
        grid=(2,),
        in_specs=[
            pl.BlockSpec((tile, 1), lambda i: (i, 0)),
            pl.BlockSpec((tile, both), lambda i: (i, 0)),
            pl.BlockSpec(back.shape, lambda i: (0, 0)),
        ],
        out_specs=pl.BlockSpec((tile, both), lambda i: (i, 0)),
        out_shape=jax.ShapeDtypeStruct((rows, both), BF16),
        compiler_params=params(32),
        cost_estimate=cost(rows * both, 4 * rows * both),
        name="finish",
    )(column, scale, back)


def per_device(grad_out, gates, expert_ids, pre_acts, w2):
    count = lax.axis_size("expert")
    me = lax.axis_index("expert")
    tokens, top = expert_ids.shape
    width = w2.shape[1]
    half = width // 2
    rows = tokens * top
    members = count // 4
    hot = 2 * rows // count
    cold = (rows - 2 * hot) // (count - 2) + 2
    cap = -(-(2 * hot + 2 * cold) // 16) * 16
    groups = [[j for j in range(count) if j & 6 == mask] for mask in PLANE]

    def exchange(chunks):
        return lax.all_to_all(
            chunks, "expert", split_axis=0, concat_axis=0, tiled=True, axis_index_groups=groups
        )

    flat_pre = pre_acts.reshape(rows, 2 * width)
    bits = [1 << b for b in reversed(range(3, count.bit_length() - 1))]
    first = [grad_out] + [swap(grad_out, bit) for bit in bits]

    own_w = lax.all_gather(w2, "dp", axis=2, tiled=True)[0]
    quarter = half // 2
    x_a1, y_b1 = swap(own_w[:quarter], X_BIT), swap(own_w[half : half + quarter], Y_BIT)
    x_a2, y_b2 = swap(own_w[quarter:half], X_BIT), swap(own_w[half + quarter :], Y_BIT)
    diag = [
        swap(jnp.concatenate([x_a1, x_a2], 0), Y_BIT),
        swap(jnp.concatenate([y_b1, y_b2], 0), X_BIT),
    ]
    x_b, y_a = swap(own_w[half:], X_BIT), swap(own_w[:half], Y_BIT)

    packed, place = pack_hidden(expert_ids, gates, flat_pre, members, cap)
    masks, path = [0] + bits, {}
    for bit in bits:
        for mask in [m for m in masks if m > bit and not m & bit and m | bit not in masks]:
            masks.append(mask | bit)
            path[mask | bit] = (mask, bit)
    info = jnp.stack([me] + [(me ^ mask) >> 3 for mask in masks]).astype(jnp.int32)

    *first, x_a1, y_b1, packed, info = lax.optimization_barrier((*first, x_a1, y_b1, packed, info))
    arrived = exchange(packed)
    blocks = dict(zip([0] + bits, first))
    for mask, (known, bit) in path.items():
        blocks[mask] = swap(blocks[known], bit)
    near = list(blocks.values())
    near[-1], x_b, y_a, *diag = lax.optimization_barrier((near[-1], x_b, y_a, *diag))
    sources = near + [swap(block, CORE_BIT) for block in near]

    slopes, x_diag, y_diag, x_own, y_own, rest = middle(
        info, sources, (own_w, x_a1, x_a2, x_b, y_a, y_b1, y_b2, *diag), arrived
    )
    back = exchange(slopes).reshape(members * cap, width)
    own, keep = keep_partials(sources, rest)

    from_x, from_y = swap(x_diag, X_BIT), swap(y_diag, Y_BIT)
    mine_x, mine_y = swap(x_own, X_BIT), swap(y_own, Y_BIT)
    mine_x, mine_y = lax.optimization_barrier((mine_x, mine_y))
    from_x, from_y = lax.optimization_barrier((from_x, from_y))
    to_y = (keep[half:].astype(F32) + from_x.astype(F32)).astype(BF16)
    to_x = (keep[:half].astype(F32) + from_y.astype(F32)).astype(BF16)
    last_y, last_x = swap(to_y, Y_BIT), swap(to_x, X_BIT)
    part = own + jnp.concatenate([mine_x, mine_y], 0).astype(F32)
    part, last_y, last_x = lax.optimization_barrier((part, last_y, last_x))
    total = part + jnp.concatenate([last_y, last_x], 0).astype(F32)
    total = lax.psum_scatter(total, "dp", scatter_dimension=1, tiled=True)

    scale, column = factors(place, gates, flat_pre, cap)
    pre_grad = finish(column, scale, back)
    return pre_grad.reshape(tokens, top, 2 * width), total[None].astype(BF16)


def solution(mesh):
    in_specs = (
        P(("groups", "expert", "dp"), None),
        P(("groups", "expert", "dp"), None),
        P(("groups", "expert", "dp"), None),
        P(("groups", "expert", "dp"), None, None),
        P("expert", None, "dp"),
    )
    out_specs = (P(("groups", "expert", "dp"), None, None), P("expert", "groups", "dp"))
    return jax.shard_map(
        per_device, mesh=mesh, in_specs=in_specs, out_specs=out_specs, check_vma=False
    )
```

```python
import jax
import jax.numpy as jnp
from jax import lax
from jax.experimental import pallas as pl
from jax.experimental.pallas import tpu as pltpu
from jax.sharding import PartitionSpec as P

X_BIT, Y_BIT, CORE_BIT = 2, 4, 1
PLANE = (0, X_BIT, Y_BIT, X_BIT | Y_BIT)
TAIL = 16
F32, BF16 = jnp.float32, jnp.bfloat16
HIGHEST = lax.Precision.HIGHEST


def params(mebibytes):
    return pltpu.CompilerParams(vmem_limit_bytes=mebibytes * 1024 * 1024)


def cost(flops, moved):
    return pl.CostEstimate(flops=flops, bytes_accessed=moved, transcendentals=0)


def swap(value, bit):
    count = lax.axis_size("expert")
    return lax.ppermute(value, "expert", [(j, j ^ bit) for j in range(count)])


def number(shape, dim):
    return lax.broadcasted_iota(jnp.int32, shape, dim)


def ones_where(condition):
    return condition.astype(F32).astype(BF16)


def dot(a, b):
    return jnp.dot(a, b, preferred_element_type=F32)


def transposed_dot(a, b):
    return lax.dot_general(a, b, (((1,), (1,)), ((), ())), preferred_element_type=F32)


VMEM = pl.BlockSpec(memory_space=pltpu.VMEM)
ANY = pl.BlockSpec(memory_space=pl.ANY)
HBM = pl.BlockSpec(memory_space=pltpu.HBM)
SMEM = pl.BlockSpec(memory_space=pltpu.SMEM)


def spread_line(tokens, rows):
    shift = (rows // tokens).bit_length() - 1
    return ones_where((number((tokens, rows), 1) >> shift) == number((tokens, rows), 0))


def column_of(values, rows):
    top, tokens = values.shape
    shift = top.bit_length() - 1
    high = values.astype(BF16)
    rest = values - high.astype(F32)
    middle = rest.astype(BF16)
    low = (rest - middle.astype(F32)).astype(BF16)
    token_of = ones_where((number((rows, tokens), 0) >> shift) == number((rows, tokens), 1))
    wide = transposed_dot(token_of, jnp.concatenate([high, middle, low], 0))
    wide = wide[:, :top] + (wide[:, top : 2 * top] + wide[:, 2 * top :])
    mine = (number((rows, top), 0) & (top - 1)) == number((rows, top), 1)
    return jnp.sum(jnp.where(mine, wide, 0.0), 1, keepdims=True)


def pack_kernel(cap, ids_ref, gates_ref, pre_hbm, out_ref, place_ref, pre, picks_ref, sem):
    copy = pltpu.make_async_copy(pre_hbm, pre, sem)
    copy.start()
    members = out_ref.shape[0]
    rows, both = pre.shape
    width = both // 2
    top, tokens = gates_ref.shape
    ids = ids_ref[...]
    member = (ids >> 3) * 2 + (ids & 1)
    hits = jnp.concatenate([(member == q).astype(F32) for q in range(members)], 0)
    size = members * top
    shift = top.bit_length() - 1
    row, col = number((size, size), 0), number((size, size), 1)
    same = (row >> shift) == (col >> shift)
    earlier = dot(ones_where(same & (col < row)), hits.astype(BF16))
    total = dot(ones_where(same), hits.astype(BF16))
    before = ones_where(number((tokens, tokens), 0) < number((tokens, tokens), 1))
    ranks = hits * (dot(total.astype(BF16), before) + earlier)
    slot = ranks[:top]
    for q in range(1, members):
        slot = slot + ranks[q * top : (q + 1) * top]
    place = member.astype(F32) * cap + slot

    gate_column = column_of(gates_ref[...], rows)
    wide = dot(jnp.concatenate([slot, member.astype(F32)], 0).astype(BF16), spread_line(tokens, rows))
    mine = (number((top, rows), 1) & (top - 1)) == number((top, rows), 0)
    slot_line = jnp.sum(jnp.where(mine, wide[:top], 0.0), 0, keepdims=True)
    member_line = jnp.sum(jnp.where(mine, wide[top:], 0.0), 0, keepdims=True)
    place_line = (member_line * cap + slot_line).astype(jnp.int32)
    for q in range(members):
        picks_ref[q * cap : (q + 1) * cap] = ones_where(
            number((cap, rows), 0) == place_line - q * cap
        )
    place_ref[...] = jnp.concatenate([slot, member.astype(F32)], 0)

    copy.wait()
    gate_pre = pre[:, :width].astype(F32)
    up_pre = pre[:, width:].astype(F32)
    hidden = (gate_pre * jax.nn.sigmoid(gate_pre) * up_pre * gate_column).astype(BF16)
    every = dot(picks_ref[...], hidden)
    tail = number((TAIL, width), 0)
    for q in range(members):
        packed = every[q * cap : (q + 1) * cap]
        first = (q >> 1) * 8 + (q & 1)
        table = [
            jnp.sum(jnp.where(ids == first + mask, slot + 1.0, 0.0), 0, keepdims=True)
            for mask in PLANE
        ]
        rest = jnp.zeros((1, width - tokens), F32)
        upper, lower = jnp.concatenate(table[:3], 1), jnp.concatenate([table[3], rest], 1)
        block = jnp.where(tail == TAIL - 2, upper, jnp.where(tail == TAIL - 1, lower, 0.0))
        out_ref[q, : cap - TAIL] = packed[: cap - TAIL].astype(BF16)
        out_ref[q, cap - TAIL :] = (packed[cap - TAIL :] + block).astype(BF16)


def pack_hidden(ids, gates, flat_pre, members, cap):
    rows, both = flat_pre.shape
    width = both // 2
    return pl.pallas_call(
        lambda *refs: pack_kernel(cap, *refs),
        in_specs=[VMEM, VMEM, HBM],
        out_specs=[VMEM] * 2,
        out_shape=[
            jax.ShapeDtypeStruct((members, cap, width), BF16),
            jax.ShapeDtypeStruct((2 * gates.shape[1], gates.shape[0]), F32),
        ],
        scratch_shapes=[
            pltpu.VMEM((rows, both), BF16),
            pltpu.VMEM((members * cap, rows), BF16),
            pltpu.SemaphoreType.DMA,
        ],
        compiler_params=params(40),
        cost_estimate=cost(2 * members * cap * rows * width, 2 * rows * both),
        name="pack_hidden",
    )(ids.T, gates.T, flat_pre)


def factors_kernel(cap, place_ref, gates_ref, pre_ref, out_ref, column_ref, gate):
    top = gates_ref.shape[0]
    rows = gate.shape[0]
    tile, both = pre_ref.shape
    width = both // 2
    step = pl.program_id(0)

    @pl.when(step == 0)
    def _():
        gate[...] = column_of(gates_ref[...], rows)
        column_ref[...] = column_of(place_ref[top:] * cap + place_ref[:top], rows).astype(jnp.int32)

    gate_pre = pre_ref[:, :width].astype(F32)
    up_pre = pre_ref[:, width:].astype(F32)
    sigma = jax.nn.sigmoid(gate_pre)
    own = gate[pl.ds(pl.multiple_of(step * tile, tile), tile), :]
    out_ref[:, :width] = (own * up_pre * (sigma * (1.0 + gate_pre * (1.0 - sigma)))).astype(BF16)
    out_ref[:, width:] = (own * (gate_pre * sigma)).astype(BF16)


def factors(place, gates, flat_pre, cap):
    rows, both = flat_pre.shape
    tile = rows // 4
    whole = lambda a: pl.BlockSpec(a.shape, lambda i: (0, 0))
    return pl.pallas_call(
        lambda *refs: factors_kernel(cap, *refs),
        grid=(4,),
        in_specs=[whole(place), whole(gates.T), pl.BlockSpec((tile, both), lambda i: (i, 0))],
        out_specs=[
            pl.BlockSpec((tile, both), lambda i: (i, 0)),
            pl.BlockSpec((rows, 1), lambda i: (0, 0)),
        ],
        out_shape=[
            jax.ShapeDtypeStruct((rows, both), BF16),
            jax.ShapeDtypeStruct((rows, 1), jnp.int32),
        ],
        scratch_shapes=[pltpu.VMEM((rows, 1), F32)],
        compiler_params=params(16),
        name="factors",
    )(place, gates.T, flat_pre)


def picks(chunk, cap, tokens):
    table = chunk[chunk.shape[0] - TAIL :].astype(F32)
    upper, lower = table[TAIL - 2 : TAIL - 1], table[TAIL - 1 :]
    row = (number((cap, tokens), 0) + 1).astype(F32)
    slots = [upper[:, e * tokens : (e + 1) * tokens] for e in range(3)] + [lower[:, :tokens]]
    return slots, row


def pick_for(chunk, me, cap, tokens):
    slots, row = picks(chunk, cap, tokens)
    parts = []
    for mask in PLANE:
        index = ((me ^ mask) >> 1) & 3
        slot = slots[0]
        for e in range(1, 4):
            slot = jnp.where(index == e, slots[e], slot)
        parts.append(ones_where(row == slot))
    return jnp.concatenate(parts, 1)


def gather_copies(sources, target, sem):
    tokens = sources[0].shape[0]
    return [
        pltpu.make_async_copy(ref, target.at[pl.ds(at * tokens, tokens), :], sem.at[at])
        for at, ref in enumerate(sources)
    ]


def place_of(info, at, blocks):
    core = info[0] & 1
    return info[1 + at % blocks] * 2 + (core if at < blocks else 1 - core)


def middle_kernel(cap, count, info, *refs):
    sources, w, refs = refs[:count], refs[count:-20], refs[-20:]
    hidden, out_ref, x_diag, y_diag, x_own, y_own, rest, *refs = refs
    grads, weights, rows, spread, pick, slopes, packed, result, sem, wsem, hsem, osem, psem = refs
    me = info[0]
    tokens = sources[0].shape[0]
    width = rows.shape[2]
    half = width // 2
    hidden_copy = pltpu.make_async_copy(hidden, rows, hsem)
    token_copies = gather_copies(sources, grads, sem)
    weight_copies, start = [], 0
    for i, ref in enumerate(w):
        weight_copies.append(
            pltpu.make_async_copy(ref, weights.at[pl.ds(start, ref.shape[0]), :], wsem.at[i])
        )
        start += ref.shape[0]
    for copy in [hidden_copy] + token_copies + weight_copies:
        copy.start()
    hidden_copy.wait()
    layout = (
        (2 * width, 2 * width + half),
        (width, 3 * width),
        (3 * width + half, width + half),
        (0, half),
    )
    places = [place_of(info, at, count // 2) for at in range(count)]
    for at in range(count):
        chunk = rows[places[at]]
        pick[at] = pick_for(chunk, me, cap, tokens)
        wide = dot(chunk.astype(F32).T.astype(BF16), pick[at]).astype(BF16)
        for e in range(4):
            for h in range(2):
                spread[pl.ds(layout[e][h], half), at * tokens : (at + 1) * tokens] = wide[
                    h * half : (h + 1) * half, e * tokens : (e + 1) * tokens
                ]
    copies = [pltpu.make_async_copy(spread.at[pl.ds(2 * width, 2 * width), :], rest, osem.at[4])]
    copies[0].start()
    for copy in token_copies:
        copy.wait()
    result[...] = dot(spread[: 2 * width], grads[...]).astype(BF16)
    for i, target in enumerate((x_diag, y_diag, x_own, y_own)):
        copy = pltpu.make_async_copy(result.at[pl.ds(i * half, half), :], target, osem.at[i])
        copy.start()
        copies.append(copy)
    for copy in weight_copies:
        copy.wait()
    for first in range(0, count, 4):
        four = transposed_dot(
            grads[first * tokens : (first + 4) * tokens], weights[...]
        ).astype(BF16)
        for at in range(first, first + 4):
            side = four[(at - first) * tokens : (at - first + 1) * tokens]
            for e in range(4):
                slopes[at, e * tokens : (e + 1) * tokens] = side[:, e * width : (e + 1) * width]
            packed[at] = dot(pick[at], slopes[at]).astype(BF16)
        for at in range(first, first + 4):
            copy = pltpu.make_async_copy(packed.at[at], out_ref.at[places[at]], psem.at[at])
            copy.start()
            copies.append(copy)
    for copy in copies:
        copy.wait()


def middle(info, sources, weights, hidden):
    count = len(sources)
    tokens, model = sources[0].shape
    _, cap, width = hidden.shape
    every = count * tokens
    return pl.pallas_call(
        lambda *refs: middle_kernel(cap, count, *refs),
        in_specs=[SMEM] + [ANY] * (count + len(weights) + 1),
        out_specs=[ANY] * 6,
        out_shape=[jax.ShapeDtypeStruct(hidden.shape, BF16)]
        + [jax.ShapeDtypeStruct((width // 2, model), BF16)] * 4
        + [jax.ShapeDtypeStruct((2 * width, every), BF16)],
        scratch_shapes=[
            pltpu.VMEM((every, model), BF16),
            pltpu.VMEM((4 * width, model), BF16),
            pltpu.VMEM(hidden.shape, BF16),
            pltpu.VMEM((4 * width, every), BF16),
            pltpu.VMEM((count, cap, 4 * tokens), BF16),
            pltpu.VMEM((count, 4 * tokens, width), BF16),
            pltpu.VMEM(hidden.shape, BF16),
            pltpu.VMEM((2 * width, model), BF16),
            pltpu.SemaphoreType.DMA((count,)),
            pltpu.SemaphoreType.DMA((len(weights),)),
            pltpu.SemaphoreType.DMA,
            pltpu.SemaphoreType.DMA((5,)),
            pltpu.SemaphoreType.DMA((count,)),
        ],
        compiler_params=params(52),
        cost_estimate=cost(2 * every * model * 6 * width, 4 * every * model),
        name="middle",
    )(info, *sources, *weights, hidden)


def keep_kernel(count, *refs):
    sources, refs = refs[:count], refs[count:]
    rest, own, keep, spread, grads, result, kept, sem, rsem, osem = refs
    width = kept.shape[0]
    rest_copy = pltpu.make_async_copy(rest, spread, rsem)
    copies = [rest_copy] + gather_copies(sources, grads, sem)
    for copy in copies:
        copy.start()
    for copy in copies:
        copy.wait()
    result[...] = dot(spread[width:], grads[...]).astype(BF16)
    keep_copy = pltpu.make_async_copy(result, keep, osem.at[0])
    keep_copy.start()
    kept[...] = dot(spread[:width], grads[...])
    own_copy = pltpu.make_async_copy(kept, own, osem.at[1])
    own_copy.start()
    keep_copy.wait()
    own_copy.wait()


def keep_partials(sources, rest):
    count = len(sources)
    tokens, model = sources[0].shape
    width, every = rest.shape[0] // 2, count * tokens
    return pl.pallas_call(
        lambda *refs: keep_kernel(count, *refs),
        in_specs=[ANY] * (count + 1),
        out_specs=[ANY] * 2,
        out_shape=[
            jax.ShapeDtypeStruct((width, model), F32),
            jax.ShapeDtypeStruct((width, model), BF16),
        ],
        scratch_shapes=[
            pltpu.VMEM((2 * width, every), BF16),
            pltpu.VMEM((every, model), BF16),
            pltpu.VMEM((width, model), BF16),
            pltpu.VMEM((width, model), F32),
            pltpu.SemaphoreType.DMA((count,)),
            pltpu.SemaphoreType.DMA,
            pltpu.SemaphoreType.DMA((2,)),
        ],
        compiler_params=params(52),
        cost_estimate=cost(2 * every * model * 2 * width, 4 * every * model),
        name="keep_partials",
    )(*sources, rest)


def finish_kernel(column_ref, factors_ref, back_ref, out_ref):
    rows, both = factors_ref.shape
    width = both // 2
    slots = back_ref.shape[0]
    pick = ones_where(number((rows, slots), 1) == column_ref[...])
    slope = dot(pick, back_ref[...])
    out_ref[:, :width] = (slope * factors_ref[:, :width].astype(F32)).astype(BF16)
    out_ref[:, width:] = (slope * factors_ref[:, width:].astype(F32)).astype(BF16)


def finish(column, scale, back):
    rows, both = scale.shape
    tile = rows // 2
    return pl.pallas_call(
        finish_kernel,
        grid=(2,),
        in_specs=[
            pl.BlockSpec((tile, 1), lambda i: (i, 0)),
            pl.BlockSpec((tile, both), lambda i: (i, 0)),
            pl.BlockSpec(back.shape, lambda i: (0, 0)),
        ],
        out_specs=pl.BlockSpec((tile, both), lambda i: (i, 0)),
        out_shape=jax.ShapeDtypeStruct((rows, both), BF16),
        compiler_params=params(32),
        cost_estimate=cost(rows * both, 4 * rows * both),
        name="finish",
    )(column, scale, back)


def per_device(grad_out, gates, expert_ids, pre_acts, w2):
    count = lax.axis_size("expert")
    me = lax.axis_index("expert")
    tokens, top = expert_ids.shape
    width = w2.shape[1]
    half = width // 2
    rows = tokens * top
    members = count // 4
    hot = 2 * rows // count
    cold = (rows - 2 * hot) // (count - 2) + 2
    cap = -(-(2 * hot + 2 * cold) // 16) * 16
    groups = [[j for j in range(count) if j & 6 == mask] for mask in PLANE]

    def exchange(chunks):
        return lax.all_to_all(
            chunks, "expert", split_axis=0, concat_axis=0, tiled=True, axis_index_groups=groups
        )

    flat_pre = pre_acts.reshape(rows, 2 * width)
    bits = [1 << b for b in reversed(range(3, count.bit_length() - 1))]
    first = [grad_out] + [swap(grad_out, bit) for bit in bits]

    own_w = lax.all_gather(w2, "dp", axis=2, tiled=True)[0]
    quarter = half // 2
    x_a1, y_b1 = swap(own_w[:quarter], X_BIT), swap(own_w[half : half + quarter], Y_BIT)
    x_a2, y_b2 = swap(own_w[quarter:half], X_BIT), swap(own_w[half + quarter :], Y_BIT)
    diag = [
        swap(jnp.concatenate([x_a1, x_a2], 0), Y_BIT),
        swap(jnp.concatenate([y_b1, y_b2], 0), X_BIT),
    ]
    x_b, y_a = swap(own_w[half:], X_BIT), swap(own_w[:half], Y_BIT)

    packed, place = pack_hidden(expert_ids, gates, flat_pre, members, cap)
    masks, path = [0] + bits, {}
    for bit in bits:
        for mask in [m for m in masks if m > bit and not m & bit and m | bit not in masks]:
            masks.append(mask | bit)
            path[mask | bit] = (mask, bit)
    info = jnp.stack([me] + [(me ^ mask) >> 3 for mask in masks]).astype(jnp.int32)

    *first, x_a1, y_b1, packed, info = lax.optimization_barrier((*first, x_a1, y_b1, packed, info))
    arrived = exchange(packed)
    blocks = dict(zip([0] + bits, first))
    for mask, (known, bit) in path.items():
        blocks[mask] = swap(blocks[known], bit)
    near = list(blocks.values())
    near[-1], x_b, y_a, *diag = lax.optimization_barrier((near[-1], x_b, y_a, *diag))
    sources = near + [swap(block, CORE_BIT) for block in near]

    slopes, x_diag, y_diag, x_own, y_own, rest = middle(
        info, sources, (own_w, x_a1, x_a2, x_b, y_a, y_b1, y_b2, *diag), arrived
    )
    back = exchange(slopes).reshape(members * cap, width)
    own, keep = keep_partials(sources, rest)

    from_x, from_y = swap(x_diag, X_BIT), swap(y_diag, Y_BIT)
    mine_x, mine_y = swap(x_own, X_BIT), swap(y_own, Y_BIT)
    mine_x, mine_y = lax.optimization_barrier((mine_x, mine_y))
    from_x, from_y = lax.optimization_barrier((from_x, from_y))
    to_y = (keep[half:].astype(F32) + from_x.astype(F32)).astype(BF16)
    to_x = (keep[:half].astype(F32) + from_y.astype(F32)).astype(BF16)
    last_y, last_x = swap(to_y, Y_BIT), swap(to_x, X_BIT)
    part = own + jnp.concatenate([mine_x, mine_y], 0).astype(F32)
    part, last_y, last_x = lax.optimization_barrier((part, last_y, last_x))
    total = part + jnp.concatenate([last_y, last_x], 0).astype(F32)
    total = lax.psum_scatter(total, "dp", scatter_dimension=1, tiled=True)

    scale, column = factors(place, gates, flat_pre, cap)
    pre_grad = finish(column, scale, back)
    return pre_grad.reshape(tokens, top, 2 * width), total[None].astype(BF16)


def solution(mesh):
    in_specs = (
        P(("groups", "expert", "dp"), None),
        P(("groups", "expert", "dp"), None),
        P(("groups", "expert", "dp"), None),
        P(("groups", "expert", "dp"), None, None),
        P("expert", None, "dp"),
    )
    out_specs = (P(("groups", "expert", "dp"), None, None), P("expert", "groups", "dp"))
    return jax.shard_map(
        per_device, mesh=mesh, in_specs=in_specs, out_specs=out_specs, check_vma=False
    )
```
